256 devices in a mesh: inner: 4 (over y), outer: 64 (over z, x, core).
Axes of the slice: x: 4, y: 4, z: 8, core: 2. Of those that a mesh axis runs over, the one named last changes fastest.
Arguments:
- queries: bfloat16 [32768, 640], P(('inner', 'outer')), may hold values from -6 to 6
- keys: bfloat16 [32768, 128], P(('inner', 'outer')), may hold values from -6 to 6
- values: bfloat16 [32768, 128], P(('inner', 'outer')), may hold values from -6 to 6
- attention_out: bfloat16 [32768, 640], P(('inner', 'outer')), may hold values from -4 to 4
- output_grad: bfloat16 [32768, 640], P(('inner', 'outer')), may hold values from -6 to 6
- log_norm: float32 [5, 32768], P(None, ('inner', 'outer')), may hold values from 3 to 6
- layer_input: bfloat16 [32768, 5120], P(('inner', 'outer'))
- doc_start: int32 [32768], P(('inner', 'outer')), may hold values from 0 to 32767, as said below
- visible_blocks: int32 [256, 5], P(('inner', 'outer')), may hold values from -1 to 255, as said below
Outputs:
- projection_grad: float32 [5120, 256], P(('inner', 'outer'))
- query_grad: bfloat16 [32768, 640], P(('inner', 'outer'))
The draws below stay inside these ranges and needn't reach their ends.
Inputs may be any that keep to these rules, and one draw needn't show every extreme that they name: doc_start[t] is the first position of the document holding position t: it is at most t, equal over one document, and a document begins where it changes. A document has at most 512 positions and one has exactly 512. `visible_blocks`: row i lists in ascending order the key blocks from the block that holds doc_start[i * 128] up to block i, followed by -1 in the slots left over; some row has no -1.
All inputs are finite; a program needn't handle non-finite values.
Results may differ from the reference program's by a relative error of at most 0.0057.
Values may be sent and summed in bfloat16 or wider, within the bound.
A program may use at most 64 MiB of HBM per device.

```python
import jax
import jax.numpy as jnp
from jax import lax

D = 5120
HQ = 5
HD = 128
TOK_DEV = 128
VIS = 5
BLOCKS = 256
TOKENS = 32768
MAXLEN = 512


def document_layout(key):
    lengths = jax.random.randint(jax.random.fold_in(key, 77), (TOKENS,), 1, MAXLEN + 1)
    lengths = lengths.at[0].set(TOK_DEV // 2).at[1].set(MAXLEN)
    starts = jnp.cumsum(lengths) - lengths
    positions = jnp.arange(TOKENS, dtype=jnp.int32)
    doc_index = jnp.searchsorted(starts, positions, side='right') - 1
    return starts[doc_index].astype(jnp.int32)


def draw_doc_start(key, part):
    first_pos = document_layout(key)
    return first_pos


def draw_visible_blocks(key, part):
    first_pos = document_layout(key)
    first_block = first_pos[::TOK_DEV] // TOK_DEV
    entries = first_block[:, None] + jnp.arange(VIS, dtype=jnp.int32)[None, :]
    block_ids = jnp.arange(BLOCKS, dtype=jnp.int32)[:, None]
    return jnp.where(entries <= block_ids, entries, -1).astype(jnp.int32)


def draw_layer_input(key, part):
    key = jax.random.fold_in(key, 5)
    scale_key, base_key = jax.random.split(key, 2)
    drift_key = jax.random.fold_in(jax.random.fold_in(key, 11), 0)
    feature_scale = jnp.exp(jax.random.uniform(scale_key, (1, D), jnp.float32, jnp.log(0.3), jnp.log(3.0)))
    block_of_row = (jnp.arange(TOKENS, dtype=jnp.int32) // TOK_DEV).astype(jnp.float32)
    ramp = (block_of_row / jnp.float32(BLOCKS - 1) - 0.5)[:, None]
    drift_dir = 6.0 * jax.random.normal(drift_key, (1, D), jnp.float32)
    result = (jax.random.normal(base_key, (TOKENS, D), jnp.float32) + ramp * drift_dir) * feature_scale
    return result.astype(jnp.bfloat16)


def level_of(own_key, extent, cuts, least, largest):
    def one(position, parts):
        heights = jax.random.uniform(jax.random.fold_in(jax.random.fold_in(own_key, 6), position), (parts,), jnp.float32, least / len(cuts), largest / len(cuts))
        return jnp.repeat(jnp.exp(heights), extent[position] // parts).reshape((-1,) + (1,) * (len(extent) - position - 1))

    level = one(*cuts[0])
    for cut in cuts[1:]:
        level = level * one(*cut)
    return level


def scatter_about(key, extent, deviation, most, cuts=(), held_as=jnp.bfloat16):
    factor_of = level_of(key, extent, cuts, -0.22, 0.18) if cuts else 1.0
    values = jax.random.normal(key, extent, jnp.float32) * deviation * factor_of
    return jnp.minimum(jnp.maximum(values, -most), most).astype(held_as)


def setup_inputs(seed: int = 0) -> dict:
    arg_keys = jax.random.split(jax.random.key(seed), 10)
    queries = scatter_about(arg_keys[0], (TOKENS, HQ * HD), 1.0, 6.0, ((0, 256),))
    keys = scatter_about(arg_keys[1], (TOKENS, HD), 1.0, 6.0, ((0, 256),))
    values = scatter_about(arg_keys[2], (TOKENS, HD), 1.0, 6.0, ((0, 256),))
    attention_out = scatter_about(arg_keys[3], (TOKENS, HQ * HD), 0.5, 4.0, ((0, 256),))
    output_grad = scatter_about(arg_keys[4], (TOKENS, HQ * HD), 1.0, 6.0, ((0, 256),))
    log_norm = jnp.clip(3.0 + 3.0 * jax.random.uniform(arg_keys[5], (HQ, TOKENS), jnp.float32) ** level_of(arg_keys[5], (HQ, TOKENS), ((1, 256),), -0.2, 0.2), 3.0, 6.0)
    layer_input = draw_layer_input(jax.random.fold_in(arg_keys[9], 71), 0)
    doc_start = draw_doc_start(jax.random.fold_in(arg_keys[9], 71), 0)
    visible_blocks = draw_visible_blocks(jax.random.fold_in(arg_keys[9], 71), 0)
    return {"queries": queries, "keys": keys, "values": values, "attention_out": attention_out, "output_grad": output_grad, "log_norm": log_norm, "layer_input": layer_input, "doc_start": doc_start, "visible_blocks": visible_blocks}


def reference(queries, keys, values, attention_out, output_grad, log_norm, layer_input, doc_start, visible_blocks):
    total_rows = queries.shape[0]
    block_rows = TOK_DEV
    num_blocks = total_rows // block_rows
    query_heads = queries.reshape(total_rows, HQ, HD)
    grad_heads = output_grad.reshape(total_rows, HQ, HD)
    out_heads = attention_out.reshape(total_rows, HQ, HD)
    row_delta = lax.optimization_barrier(jnp.sum(grad_heads.astype(jnp.float32) * out_heads.astype(jnp.float32), axis=2)).T
    pad_rows = (VIS - 1) * block_rows
    key_pad = jnp.concatenate([jnp.zeros((pad_rows, HD), jnp.bfloat16), keys], axis=0)
    value_pad = jnp.concatenate([jnp.zeros((pad_rows, HD), jnp.bfloat16), values], axis=0)
    inv_scale = 1.0 / jnp.sqrt(jnp.float32(HD))
    window = VIS * block_rows

    def one_block(carry, block_index):
        key_sum, value_sum = carry
        first_row = (block_index * block_rows).astype(jnp.int32)
        query_rows = lax.dynamic_slice_in_dim(query_heads, first_row, block_rows, 0).astype(jnp.float32)
        grad_rows = lax.dynamic_slice_in_dim(grad_heads, first_row, block_rows, 0).astype(jnp.float32)
        norm_rows = lax.dynamic_slice_in_dim(log_norm, first_row, block_rows, 1)
        delta_rows = lax.dynamic_slice_in_dim(row_delta, first_row, block_rows, 1)
        start_rows = lax.dynamic_slice_in_dim(doc_start, first_row, block_rows, 0)
        key_rows = lax.dynamic_slice_in_dim(key_pad, first_row, window, 0).astype(jnp.float32)
        value_rows = lax.dynamic_slice_in_dim(value_pad, first_row, window, 0).astype(jnp.float32)
        key_pos = (first_row - pad_rows + jnp.arange(window, dtype=jnp.int32)).astype(jnp.int32)
        key_block = jnp.floor_divide(key_pos, block_rows)
        listed = lax.dynamic_index_in_dim(visible_blocks, block_index, 0, keepdims=False)
        in_list = jnp.any(key_block[:, None] == listed[None, :], axis=1) & (key_pos >= 0)
        query_pos = first_row + jnp.arange(block_rows, dtype=jnp.int32)
        allowed = in_list[None, :] & (key_pos[None, :] >= start_rows[:, None]) & (key_pos[None, :] <= query_pos[:, None])
        scores = jnp.einsum('thd,ud->htu', query_rows, key_rows) * inv_scale
        prob_full = jnp.where(allowed[None], jnp.exp(scores - norm_rows[:, :, None]), jnp.float32(0.0))
        prob_half = prob_full.astype(jnp.bfloat16)
        prob_grad = jnp.einsum('thd,ud->htu', grad_rows, value_rows)
        score_grad = (prob_full * (prob_grad - delta_rows[:, :, None]) * inv_scale).astype(jnp.bfloat16)
        score_wide = score_grad.astype(jnp.float32)
        query_part = jnp.einsum('htu,ud->thd', score_wide, key_rows).reshape(block_rows, HQ * HD).astype(jnp.bfloat16)
        key_part = jnp.einsum('htu,thd->ud', score_wide, query_rows)
        value_part = jnp.einsum('htu,thd->ud', prob_half.astype(jnp.float32), grad_rows)
        key_sum = lax.dynamic_update_slice_in_dim(key_sum, lax.dynamic_slice_in_dim(key_sum, first_row, window, 0) + key_part, first_row, 0)
        value_sum = lax.dynamic_update_slice_in_dim(value_sum, lax.dynamic_slice_in_dim(value_sum, first_row, window, 0) + value_part, first_row, 0)
        return ((key_sum, value_sum), query_part)
    empty = jnp.zeros((pad_rows + total_rows, HD), jnp.float32)
    (key_sum, value_sum), query_parts = lax.scan(one_block, (empty, empty), jnp.arange(num_blocks, dtype=jnp.int32))
    query_grad = query_parts.reshape(total_rows, HQ * HD)
    key_grad = key_sum[pad_rows:].astype(jnp.bfloat16)
    value_grad = value_sum[pad_rows:].astype(jnp.bfloat16)
    all_grads = jnp.concatenate([key_grad, value_grad], axis=1)
    weight_sum = jnp.dot(layer_input.T, all_grads, preferred_element_type=jnp.float32)
    square_total = jnp.sum(weight_sum * weight_sum)
    limit = jnp.sqrt(jnp.float32(D * 2 * HD))
    clip_factor = jnp.minimum(jnp.float32(1.0), limit / (jnp.sqrt(square_total) + 1e-06))
    return (weight_sum * clip_factor, query_grad)
```

```python
import math

import jax
import jax.numpy as jnp
from jax import lax
from jax.experimental import pallas as pl
from jax.experimental.pallas import tpu as pltpu
from jax.sharding import PartitionSpec as P

D = 5120
HD = 128
HQ = 5
T = 128
Y, Z, X, C = 4, 8, 4, 2
N = Y * Z * X * C
DY = D // Y
DC = DY // C
ROWS = D // N
WIN = 24
FAR = 1.0e9
MESH = pl.DeviceIdType.MESH
f32, bf16 = jnp.float32, jnp.bfloat16
SCALE = 1.0 / math.sqrt(HD)
LOG2E = math.log2(math.e)


def place(y, z, x, c):
    return {"inner": y, "outer": (z * X + x) * C + c}


def dot(a, b, dims):
    return lax.dot_general(a, b, (dims, ((), ())), preferred_element_type=f32)


def kernel(
    q_hbm,
    k_hbm,
    v_hbm,
    o_hbm,
    do_hbm,
    lse_ref,
    x_hbm,
    start_ref,
    vis_ref,
    w_ref,
    dq_ref,
    q_all,
    do_all,
    o_own,
    kbuf,
    vbuf,
    stat,
    ds_buf,
    ret_send,
    ret_recv,
    dq_part,
    dq_recv,
    x_recv,
    xt,
    g_all,
    acc,
    rs_send,
    rs_recv,
    wsum,
    sq1,
    sq2,
    load_sem,
    qx_s,
    qx_r,
    kv_s,
    kv_r,
    ret_s,
    ret_r,
    x_s,
    x_r,
    g_s,
    g_r,
    fwd_s,
    dq_s,
    dq_r,
    rs_s,
    rs_r,
    sq_s,
    sq_r,
):
    y = lax.axis_index("inner")
    outer = lax.axis_index("outer")
    z = outer // (X * C)
    x = (outer // C) % X
    c = outer % C
    other = 1 - c
    block = y * (Z * X * C) + outer
    sib = place(y, z, x, other)
    rs_core = z // (Z // C)
    self_rs = rs_core == c

    def block_at(step):
        b = lax.rem(block + (step + N), N)
        return {"inner": b // (Z * X * C), "outer": lax.rem(b, Z * X * C)}

    def send(src, dst, ssem, rsem, device):
        copy = pltpu.make_async_remote_copy(
            src_ref=src, dst_ref=dst, send_sem=ssem, recv_sem=rsem, device_id=device, device_id_type=MESH
        )
        return copy

    loads = [
        pltpu.make_async_copy(do_hbm, do_all.at[c], load_sem.at[0]),
        pltpu.make_async_copy(o_hbm, o_own, load_sem.at[1]),
        pltpu.make_async_copy(q_hbm, q_all.at[c], load_sem.at[2]),
        pltpu.make_async_copy(k_hbm, kbuf.at[0], load_sem.at[3]),
        pltpu.make_async_copy(v_hbm, vbuf.at[0], load_sem.at[4]),
    ]
    for load in loads:
        load.start()

    barrier = pltpu.get_barrier_semaphore()

    def greet(device):
        pl.semaphore_signal(barrier, inc=1, device_id=device, device_id_type=MESH)

    greet(sib)
    for step in (-4, -2, 2, 4):
        greet(block_at(step))
    for dy in range(1, Y):
        for cc in range(C):
            greet(place(lax.rem(y + dy, Y), z, x, cc))

    def greet_rs(i, _):
        zz, xx = i // X, lax.rem(i, X)

        @pl.when(jnp.logical_not((zz == z) & (xx == x) & self_rs))
        def _():
            greet(place(y, zz, xx, rs_core))

        return 0

    lax.fori_loop(0, Z * X, greet_rs, 0)

    def greet_xy(i, _):
        greet(place(lax.rem(y + i // X, Y), z, lax.rem(x + lax.rem(i, X), X), c))
        return 0

    lax.fori_loop(1, Y * X, greet_xy, 0)

    def greet_zc(i, _):
        greet(place(y, lax.rem(z + i // C, Z), x, lax.rem(c + lax.rem(i, C), C)))
        return 0

    lax.fori_loop(1, Z * C, greet_zc, 0)

    loads[0].wait()
    loads[1].wait()
    for h in range(HQ):
        cols = pl.ds(h * HD, HD)
        prod = do_all[c, :, cols].astype(f32) * o_own[:, cols].astype(f32)
        stat[c, pl.ds(h, 1), :] = jnp.sum(prod.T, axis=0, keepdims=True)
    stat[c, pl.ds(HQ, HQ), :] = lse_ref[...] * LOG2E
    first = start_ref[...].astype(f32)
    for d in range(5):
        kb = block - d
        wanted = jnp.where(kb >= 0, kb, -7)
        hit = jnp.max(jnp.where(vis_ref[...] == wanted, 1.0, 0.0), axis=1, keepdims=True)
        stat[c, pl.ds(10 + d, 1), :] = jnp.where(hit > 0.5, first, FAR)
    stat[c, pl.ds(15, 1), :] = jnp.full((1, T), FAR, f32)

    waits = 1 + 4 + 6 + (Y * X - 1) + (Z * C - 1) + Z * X
    pl.semaphore_wait(barrier, waits - jnp.where(self_rs, 1, 0))

    cp_q = send(q_hbm, q_all.at[c], qx_s.at[0], qx_r.at[0], sib)
    cp_do = send(do_hbm, do_all.at[c], qx_s.at[1], qx_r.at[1], sib)
    cp_st = send(stat.at[c], stat.at[c], qx_s.at[2], qx_r.at[2], sib)
    cp_kv = []
    for j in (1, 2):
        cp_kv.append(send(k_hbm, kbuf.at[j], kv_s.at[2 * j - 2], kv_r.at[2 * j - 2], block_at(2 * j)))
        cp_kv.append(send(v_hbm, vbuf.at[j], kv_s.at[2 * j - 1], kv_r.at[2 * j - 1], block_at(2 * j)))
    for copy in cp_kv:
        copy.start()
    cp_st.start()
    cp_q.start()
    cp_do.start()

    def x_cols(yy, cc):
        return x_hbm.at[:, pl.ds(pl.multiple_of(yy * DY + cc * DC, HD), DC)]

    x_own = pltpu.make_async_copy(x_cols(y, c), x_recv.at[y, pl.ds(pl.multiple_of(c * T, T), T)], load_sem.at[5])
    x_own.start()
    my_rows = x_recv.at[y, pl.ds(pl.multiple_of(c * T, T), T)]
    cp_x = []
    for i, (dy, dc) in enumerate([(0, 1), (1, 0), (3, 0), (1, 1), (3, 1), (2, 0), (2, 1)]):
        yy, cc = lax.rem(y + dy, Y), lax.rem(c + dc, C)
        copy = send(x_cols(yy, cc), my_rows, x_s.at[i], x_r.at[i], place(yy, z, x, cc))
        copy.start()
        cp_x.append(copy)

    for load in loads[2:]:
        load.wait()
    cp_q.wait_recv()
    cp_do.wait_recv()
    cp_st.wait_recv()

    def row(r):
        return jnp.concatenate([stat[0, pl.ds(r, 1), :], stat[1, pl.ds(r, 1), :]], axis=1)

    iota_u = lax.broadcasted_iota(jnp.int32, (T, 2 * T), 0)
    iota_t = lax.broadcasted_iota(jnp.int32, (T, 2 * T), 1)
    pair_first = (block - c) * T
    query_pos = pair_first + iota_t
    own_key = own_value = None
    for j in range(3):
        if j > 0:
            cp_kv[2 * j - 2].wait_recv()
            cp_kv[2 * j - 1].wait_recv()
        key_pos = (block - 2 * j) * T + iota_u
        lows = []
        for i in range(C):
            d0, d1 = i + 2 * j, i - 1 + 2 * j
            at0, at1 = 10 + min(d0, 5), 10 + (d1 if d1 >= 0 else 5)
            lows.append(jnp.where(c == 0, stat[i, pl.ds(at0, 1), :], stat[i, pl.ds(at1, 1), :]))
        low = jnp.concatenate(lows, axis=1)
        allowed = (key_pos.astype(f32) >= low) & (key_pos <= query_pos)
        key_rows, value_rows = kbuf[j], vbuf[j]
        key_part = jnp.zeros((T, HD), f32)
        value_part = jnp.zeros((T, HD), f32)
        for h in range(HQ):
            cols = pl.ds(h * HD, HD)
            qh = q_all[:, :, cols].reshape(2 * T, HD)
            doh = do_all[:, :, cols].reshape(2 * T, HD)
            s = dot(key_rows, qh, ((1,), (1,)))
            prob = jnp.where(allowed, jnp.exp2(s * (SCALE * LOG2E) - row(HQ + h)), 0.0)
            dp = dot(value_rows, doh, ((1,), (1,)))
            ds = (prob * (dp - row(h)) * SCALE).astype(bf16)
            ds_buf[h, pl.ds(j * T, T), :] = ds
            key_part += dot(ds, qh, ((1,), (0,)))
            value_part += dot(prob.astype(bf16), doh, ((1,), (0,)))
        if j == 0:
            own_key, own_value = key_part, value_part
            wsum[:, pl.ds(0, HD)] = own_key
            wsum[:, pl.ds(HD, HD)] = own_value
        else:
            ret_send[j - 1, :, pl.ds(0, HD)] = key_part.astype(bf16)
            ret_send[j - 1, :, pl.ds(HD, HD)] = value_part.astype(bf16)
            send(
                ret_send.at[j - 1], ret_recv.at[j - 1], ret_s.at[j - 1], ret_r.at[j - 1], block_at(-2 * j)
            ).start()

    key_cat = kbuf[...].reshape(3 * T, HD)
    for h in range(HQ):
        part = dot(ds_buf[h], key_cat, ((0,), (0,)))
        dq_part[0, :, pl.ds(h * HD, HD)] = part[:T]
        dq_part[1, :, pl.ds(h * HD, HD)] = part[T:]
    cp_dq = send(dq_part.at[other], dq_recv, dq_s.at[0], dq_r.at[0], sib)
    cp_dq.start()

    x_own.wait()
    for copy in cp_x:
        copy.wait_recv()
    for yy in range(Y):
        xt[yy] = x_recv[yy].T

    rets = []
    for j in (1, 2):
        copy = send(ret_send.at[j - 1], ret_recv.at[j - 1], ret_s.at[j - 1], ret_r.at[j - 1], block_at(-2 * j))
        copy.wait_recv()
        rets.append(copy)
    mine = pl.ds(pl.multiple_of(c * T, T), T)
    theirs = pl.ds(pl.multiple_of(other * T, T), T)
    g_all[y, mine, :] = (wsum[...] + ret_recv[0].astype(f32) + ret_recv[1].astype(f32)).astype(bf16)
    cp_g = []
    for i, dy in enumerate((2, 1, 3)):
        copy = send(g_all.at[y, mine], g_all.at[y, mine], g_s.at[i], g_r.at[i], place(lax.rem(y + dy, Y), z, x, c))
        copy.start()
        cp_g.append(copy)
    cp_sib = send(g_all.at[y, mine], g_all.at[y, mine], g_s.at[3], g_r.at[3], sib)
    cp_sib.start()

    cp_dq.wait_recv()
    dq_ref[...] = (dq_part[c] + dq_recv[...]).astype(bf16)

    cp_sib.wait_recv()
    acc[...] = dot(xt[y], g_all[y], ((1,), (0,)))
    fwds = []
    for i, dy in ((1, 1), (2, 3), (0, 2)):
        from_y = lax.rem(y + Y - dy, Y)
        cp_g[i].wait_recv()
        fwd = send(g_all.at[from_y, mine], g_all.at[from_y, mine], fwd_s.at[i], fwd_s.at[3 + i], sib)
        fwd.start()
        fwds.append(fwd)
    for n, dy in enumerate((1, 3)):
        from_y = lax.rem(y + Y - dy, Y)
        fwds[n].wait_recv()
        acc[...] += dot(xt[from_y], g_all[from_y], ((1,), (0,)))
    last_y = lax.rem(y + 2, Y)
    fwds[2].wait_recv()
    part_rows = DC // 4
    slot = z * X + x
    for kz in range(4):
        rows = pl.ds(kz * part_rows, part_rows)
        acc[rows, :] += dot(xt[last_y, rows, :], g_all[last_y], ((1,), (0,)))
        for kx in range(X):
            for kc in range(C):
                at = kz * part_rows + kx * (C * ROWS) + kc * (C * ROWS - WIN)
                n = (kz * X + kx) * C + kc
                rs_send[n] = jnp.concatenate(
                    [acc[pl.ds(at, WIN), pl.ds(0, HD)], acc[pl.ds(at, WIN), pl.ds(HD, HD)]], axis=0
                ).astype(bf16)
        for kx in range(X):
            for kc in range(C):
                n = (kz * X + kx) * C + kc
                zz = c * (Z // C) + kz
                is_self = (zz == z) & (kx == x) & (kc == c)

                @pl.when(is_self)
                def _():
                    pltpu.make_async_copy(rs_send.at[n], rs_recv.at[slot], rs_r.at[0]).start()

                @pl.when(jnp.logical_not(is_self))
                def _():
                    send(rs_send.at[n], rs_recv.at[slot], rs_s.at[0], rs_r.at[0], place(y, zz, kx, kc)).start()

    send(rs_send, rs_recv, rs_s.at[0], rs_r.at[0], sib).wait_recv()
    total = rs_recv[0].astype(f32)
    for n in range(1, Z * X):
        total += rs_recv[n].astype(f32)
    wsum[pl.ds(0, 2 * WIN), pl.ds(0, HD)] = total
    low = jnp.concatenate([wsum[pl.ds(0, ROWS), pl.ds(0, HD)], wsum[pl.ds(WIN, ROWS), pl.ds(0, HD)]], axis=1)
    high = jnp.concatenate(
        [wsum[pl.ds(WIN - ROWS, ROWS), pl.ds(0, HD)], wsum[pl.ds(2 * WIN - ROWS, ROWS), pl.ds(0, HD)]], axis=1
    )
    rows_sum = jnp.where(c == 0, low, high)

    squares = jnp.sum(rows_sum * rows_sum, axis=0, keepdims=True)
    lane = squares[:, :HD] + squares[:, HD:]
    sq1[0] = jnp.broadcast_to(lane, (8, HD))

    def send_xy(i, _):
        to = place(lax.rem(y + i // X, Y), z, lax.rem(x + lax.rem(i, X), X), c)
        send(sq1.at[0], sq1.at[i], sq_s.at[0], sq_r.at[0], to).start()
        return 0

    lax.fori_loop(1, Y * X, send_xy, 0)
    send(sq1.at[pl.ds(1, Y * X - 1)], sq1.at[pl.ds(1, Y * X - 1)], sq_s.at[0], sq_r.at[0], sib).wait_recv()
    sq2[0] = jnp.sum(sq1[...], axis=0)

    def send_zc(i, _):
        to = place(y, lax.rem(z + i // C, Z), x, lax.rem(c + lax.rem(i, C), C))
        send(sq2.at[0], sq2.at[i], sq_s.at[1], sq_r.at[1], to).start()
        return 0

    lax.fori_loop(1, Z * C, send_zc, 0)
    send(sq2.at[pl.ds(1, Z * C - 1)], sq2.at[pl.ds(1, Z * C - 1)], sq_s.at[1], sq_r.at[1], sib).wait_recv()
    lanes = jnp.sum(sq2[...], axis=0)
    square_total = jnp.sum(lanes[0:1], axis=1, keepdims=True)
    limit = math.sqrt(D * 2 * HD)
    clip = jnp.minimum(1.0, limit / (jnp.sqrt(square_total) + 1e-6))
    w_ref[...] = rows_sum * clip

    for copy in [cp_q, cp_do, cp_st, *cp_kv, *cp_x, *rets, cp_dq, *cp_g, cp_sib, *fwds]:
        copy.wait_send()

    @pl.when(self_rs)
    def _():
        part = pl.ds(0, Z * X - 1)
        send(rs_send.at[part], rs_recv.at[part], rs_s.at[0], rs_r.at[0], sib).wait_send()

    @pl.when(jnp.logical_not(self_rs))
    def _():
        send(rs_send, rs_recv, rs_s.at[0], rs_r.at[0], sib).wait_send()

    send(sq1.at[pl.ds(1, Y * X - 1)], sq1.at[pl.ds(1, Y * X - 1)], sq_s.at[0], sq_r.at[0], sib).wait_send()
    send(sq2.at[pl.ds(1, Z * C - 1)], sq2.at[pl.ds(1, Z * C - 1)], sq_s.at[1], sq_r.at[1], sib).wait_send()


def on_device(queries, keys, values, attention_out, output_grad, log_norm, layer_input, doc_start, visible_blocks):
    hbm = pl.BlockSpec(memory_space=pl.ANY)
    vmem = pl.BlockSpec(memory_space=pltpu.VMEM)
    dma = pltpu.SemaphoreType.DMA
    return pl.pallas_call(
        kernel,
        out_shape=(jax.ShapeDtypeStruct((ROWS, 2 * HD), f32), jax.ShapeDtypeStruct((T, HQ * HD), bf16)),
        in_specs=[hbm, hbm, hbm, hbm, hbm, vmem, hbm, vmem, vmem],
        out_specs=(vmem, vmem),
        scratch_shapes=[
            pltpu.VMEM((C, T, HQ * HD), bf16),
            pltpu.VMEM((C, T, HQ * HD), bf16),
            pltpu.VMEM((T, HQ * HD), bf16),
            pltpu.VMEM((3, T, HD), bf16),
            pltpu.VMEM((3, T, HD), bf16),
            pltpu.VMEM((C, 16, T), f32),
            pltpu.VMEM((HQ, 3 * T, 2 * T), bf16),
            pltpu.VMEM((2, T, 2 * HD), bf16),
            pltpu.VMEM((2, T, 2 * HD), bf16),
            pltpu.VMEM((C, T, HQ * HD), f32),
            pltpu.VMEM((T, HQ * HD), f32),
            pltpu.VMEM((Y, C * T, DC), bf16),
            pltpu.VMEM((Y, DC, C * T), bf16),
            pltpu.VMEM((Y, C * T, 2 * HD), bf16),
            pltpu.VMEM((DC, 2 * HD), f32),
            pltpu.VMEM((Z * X, 2 * WIN, HD), bf16),
            pltpu.VMEM((Z * X, 2 * WIN, HD), bf16),
            pltpu.VMEM((T, 2 * HD), f32),
            pltpu.VMEM((Y * X, 8, HD), f32),
            pltpu.VMEM((Z * C, 8, HD), f32),
            dma((6,)),
            dma((3,)),
            dma((3,)),
            dma((4,)),
            dma((4,)),
            dma((2,)),
            dma((2,)),
            dma((7,)),
            dma((7,)),
            dma((4,)),
            dma((4,)),
            dma((6,)),
            dma((1,)),
            dma((1,)),
            dma((1,)),
            dma((1,)),
            dma((2,)),
            dma((2,)),
        ],
        compiler_params=pltpu.CompilerParams(
            collective_id=0, has_side_effects=True, vmem_limit_bytes=40 * 2**20
        ),
        name="clip_attention_backward",
    )(
        queries,
        keys,
        values,
        attention_out,
        output_grad,
        log_norm,
        layer_input,
        doc_start.reshape(1, T),
        visible_blocks,
    )


def solution(mesh):
    both = ("inner", "outer")
    return jax.shard_map(
        on_device,
        mesh=mesh,
        in_specs=(
            P(both, None),
            P(both, None),
            P(both, None),
            P(both, None),
            P(both, None),
            P(None, both),
            P(both, None),
            P(both),
            P(both, None),
        ),
        out_specs=(P(both, None), P(both, None)),
        check_vma=False,
    )
```

```python
import math

import jax
import jax.numpy as jnp
from jax import lax
from jax.experimental import pallas as pl
from jax.experimental.pallas import tpu as pltpu
from jax.sharding import PartitionSpec as P

D = 5120
HD = 128
HQ = 5
T = 128
Y, Z, X, C = 4, 8, 4, 2
N = Y * Z * X * C
DY = D // Y
DC = DY // C
ROWS = D // N
PAIR = C * ROWS
FAR = 1.0e9
MESH = pl.DeviceIdType.MESH
f32, bf16 = jnp.float32, jnp.bfloat16
SCALE = 1.0 / math.sqrt(HD)
LOG2E = math.log2(math.e)


def place(y, z, x, c):
    return {"inner": y, "outer": (z * X + x) * C + c}


def dot(a, b, dims):
    return lax.dot_general(a, b, (dims, ((), ())), preferred_element_type=f32)


def kernel(
    q_hbm,
    k_hbm,
    v_hbm,
    o_hbm,
    do_hbm,
    lse_hbm,
    x_hbm,
    start_hbm,
    vis_hbm,
    w_ref,
    dq_ref,
    lse_ref,
    start_ref,
    vis_ref,
    q_all,
    do_all,
    o_own,
    kbuf,
    vbuf,
    stat,
    ds_buf,
    ret_send,
    ret_recv,
    dq_part,
    dq_recv,
    x_recv,
    xt,
    g_all,
    acc,
    rs_send,
    rs_recv,
    own,
    wsum,
    sq1,
    sq2,
    load_sem,
    qx_s,
    qx_r,
    kv_s,
    kv_r,
    ret_s,
    ret_r,
    x_s,
    x_r,
    g_s,
    g_r,
    fwd_s,
    dq_s,
    dq_r,
    rs_s,
    rs_r,
    w_s,
    w_r,
    sq_s,
    sq_r,
):
    y = lax.axis_index("inner")
    outer = lax.axis_index("outer")
    z = outer // (X * C)
    x = (outer // C) % X
    c = outer % C
    other = 1 - c
    block = y * (Z * X * C) + outer
    sib = place(y, z, x, other)
    taker = z // (Z // C) == c
    one = jnp.where(taker, 1, 0)

    def block_at(step):
        b = lax.rem(block + (step + N), N)
        return {"inner": b // (Z * X * C), "outer": lax.rem(b, Z * X * C)}

    def send(src, dst, ssem, rsem, device):
        copy = pltpu.make_async_remote_copy(
            src_ref=src, dst_ref=dst, send_sem=ssem, recv_sem=rsem, device_id=device, device_id_type=MESH
        )
        return copy

    late = []
    loads = [
        pltpu.make_async_copy(do_hbm, do_all.at[c], load_sem.at[0]),
        pltpu.make_async_copy(o_hbm, o_own, load_sem.at[1]),
        pltpu.make_async_copy(q_hbm, q_all.at[c], load_sem.at[2]),
        pltpu.make_async_copy(k_hbm, kbuf.at[0], load_sem.at[3]),
        pltpu.make_async_copy(v_hbm, vbuf.at[0], load_sem.at[4]),
        pltpu.make_async_copy(lse_hbm, lse_ref, load_sem.at[6]),
        pltpu.make_async_copy(start_hbm, start_ref, load_sem.at[7]),
        pltpu.make_async_copy(vis_hbm, vis_ref, load_sem.at[8]),
    ]
    for load in loads:
        load.start()

    barrier = pltpu.get_barrier_semaphore()

    def greet(device):
        pl.semaphore_signal(barrier, inc=1, device_id=device, device_id_type=MESH)

    def greet_zx(i, _):
        zz, xx = lax.rem(z + (Z // 2) + i // X, Z), lax.rem(x + 2 + lax.rem(i, X), X)

        @pl.when((zz != z) | (xx != x))
        def _():
            greet(place(y, zz, xx, c))

        return 0

    def greet_xy(i, _):
        greet(place(lax.rem(y + i // X, Y), z, lax.rem(x + lax.rem(i, X), X), c))
        return 0

    def greet_z(zz, _):
        cc = zz // (Z // C)

        @pl.when((zz != z) | (cc != c))
        def _():
            greet(place(y, zz, x, cc))

        return 0

    @pl.when(taker)
    def _():
        lax.fori_loop(0, Z * X, greet_zx, 0)

    lax.fori_loop(0, Z, greet_z, 0)

    @pl.when(taker)
    def _():
        lax.fori_loop(1, Y * X, greet_xy, 0)

    for step in (-4, 4, -2, 2):
        greet(block_at(step))
    for dy in (2, 1, 3):
        for cc in range(C):
            greet(place(lax.rem(y + dy, Y), z, x, cc))
    greet(sib)

    for i in (0, 1, 5, 6, 7):
        loads[i].wait()
    for h in range(HQ):
        cols = pl.ds(h * HD, HD)
        prod = do_all[c, :, cols].astype(f32) * o_own[:, cols].astype(f32)
        stat[c, pl.ds(h, 1), :] = jnp.sum(prod.T, axis=0, keepdims=True)
    stat[c, pl.ds(HQ, HQ), :] = lse_ref[...] * LOG2E
    first = start_ref[...].astype(f32)
    for d in range(5):
        kb = block - d
        wanted = jnp.where(kb >= 0, kb, -7)
        hit = jnp.max(jnp.where(vis_ref[...] == wanted, 1.0, 0.0), axis=1, keepdims=True)
        stat[c, pl.ds(10 + d, 1), :] = jnp.where(hit > 0.5, first, FAR)
    stat[c, pl.ds(15, 1), :] = jnp.full((1, T), FAR, f32)

    always = 1 + 4 + 2 * (Y - 1) + Z // C * X
    pl.semaphore_wait(barrier, always + one * (Y * X - 1 + Z * C - 1 - 1))

    cp_q = send(q_hbm, q_all.at[c], qx_s.at[0], qx_r.at[0], sib)
    cp_do = send(do_hbm, do_all.at[c], qx_s.at[1], qx_r.at[1], sib)
    cp_st = send(stat.at[c], stat.at[c], qx_s.at[2], qx_r.at[2], sib)
    cp_kv = []
    for j in (1, 2):
        cp_kv.append(send(k_hbm, kbuf.at[j], kv_s.at[2 * j - 2], kv_r.at[2 * j - 2], block_at(2 * j)))
        cp_kv.append(send(v_hbm, vbuf.at[j], kv_s.at[2 * j - 1], kv_r.at[2 * j - 1], block_at(2 * j)))
    for copy in cp_kv:
        copy.start()
    cp_st.start()
    cp_q.start()
    cp_do.start()

    def x_cols(yy, cc):
        return x_hbm.at[:, pl.ds(pl.multiple_of(yy * DY + cc * DC, HD), DC)]

    x_own = pltpu.make_async_copy(x_cols(y, c), x_recv.at[y, pl.ds(pl.multiple_of(c * T, T), T)], load_sem.at[5])
    x_own.start()
    my_rows = x_recv.at[y, pl.ds(pl.multiple_of(c * T, T), T)]
    cp_x = []
    for i, (dy, dc) in enumerate([(0, 1), (1, 0), (3, 0), (1, 1), (3, 1), (2, 0), (2, 1)]):
        yy, cc = lax.rem(y + dy, Y), lax.rem(c + dc, C)
        copy = send(x_cols(yy, cc), my_rows, x_s.at[i], x_r.at[i], place(yy, z, x, cc))
        copy.start()
        cp_x.append(copy)

    for load in loads[2:5]:
        load.wait()
    cp_q.wait_recv()
    cp_do.wait_recv()
    cp_st.wait_recv()

    def row(r):
        return jnp.concatenate([stat[0, pl.ds(r, 1), :], stat[1, pl.ds(r, 1), :]], axis=1)

    iota_u = lax.broadcasted_iota(jnp.int32, (T, 2 * T), 0)
    iota_t = lax.broadcasted_iota(jnp.int32, (T, 2 * T), 1)
    pair_first = (block - c) * T
    query_pos = pair_first + iota_t
    cp_ret = []
    for j in range(3):
        if j > 0:
            cp_kv[2 * j - 2].wait_recv()
            cp_kv[2 * j - 1].wait_recv()
        key_pos = (block - 2 * j) * T + iota_u
        lows = []
        for i in range(C):
            d0, d1 = i + 2 * j, i - 1 + 2 * j
            at0, at1 = 10 + min(d0, 5), 10 + (d1 if d1 >= 0 else 5)
            lows.append(jnp.where(c == 0, stat[i, pl.ds(at0, 1), :], stat[i, pl.ds(at1, 1), :]))
        low = jnp.concatenate(lows, axis=1)
        allowed = (key_pos.astype(f32) >= low) & (key_pos <= query_pos)
        key_rows, value_rows = kbuf[j], vbuf[j]
        key_part = jnp.zeros((T, HD), f32)
        value_part = jnp.zeros((T, HD), f32)
        for h in range(HQ):
            cols = pl.ds(h * HD, HD)
            qh = q_all[:, :, cols].reshape(2 * T, HD)
            doh = do_all[:, :, cols].reshape(2 * T, HD)
            s = dot(key_rows, qh, ((1,), (1,)))
            prob = jnp.where(allowed, jnp.exp2(s * (SCALE * LOG2E) - row(HQ + h)), 0.0)
            dp = dot(value_rows, doh, ((1,), (1,)))
            ds = (prob * (dp - row(h)) * SCALE).astype(bf16)
            ds_buf[h, pl.ds(j * T, T), :] = ds
            key_part += dot(ds, qh, ((1,), (0,)))
            value_part += dot(prob.astype(bf16), doh, ((1,), (0,)))
        if j == 0:
            own[:, pl.ds(0, HD)] = key_part
            own[:, pl.ds(HD, HD)] = value_part
        else:
            ret_send[j - 1, :, pl.ds(0, HD)] = key_part.astype(bf16)
            ret_send[j - 1, :, pl.ds(HD, HD)] = value_part.astype(bf16)
            copy = send(ret_send.at[j - 1], ret_recv.at[j - 1], ret_s.at[j - 1], ret_r.at[j - 1], block_at(-2 * j))
            copy.start()
            cp_ret.append(copy)

    key_cat = kbuf[...].reshape(3 * T, HD)
    for h in range(HQ):
        part = dot(ds_buf[h], key_cat, ((0,), (0,)))
        dq_part[0, :, pl.ds(h * HD, HD)] = part[:T]
        dq_part[1, :, pl.ds(h * HD, HD)] = part[T:]
    cp_dq = send(dq_part.at[other], dq_recv, dq_s.at[0], dq_r.at[0], sib)
    cp_dq.start()

    for copy in cp_ret:
        copy.wait_recv()
    mine = pl.ds(pl.multiple_of(c * T, T), T)
    g_all[y, mine, :] = (own[...] + ret_recv[0].astype(f32) + ret_recv[1].astype(f32)).astype(bf16)
    cp_g = []
    for i, dy in enumerate((2, 1, 3)):
        copy = send(g_all.at[y, mine], g_all.at[y, mine], g_s.at[i], g_r.at[i], place(lax.rem(y + dy, Y), z, x, c))
        copy.start()
        cp_g.append(copy)
    cp_sib = send(g_all.at[y, mine], g_all.at[y, mine], g_s.at[3], g_r.at[3], sib)
    cp_sib.start()

    cp_dq.wait_recv()
    dq_ref[...] = (dq_part[c] + dq_recv[...]).astype(bf16)

    def from_y(dy):
        return lax.rem(y + Y - dy, Y)

    def pass_on(i, dy):
        cp_g[i].wait_recv()
        part = g_all.at[from_y(dy), mine]
        fwd = send(part, part, fwd_s.at[i], fwd_s.at[3 + i], sib)
        fwd.start()
        return fwd

    x_own.wait()
    cp_x[0].wait_recv()
    xt[y] = x_recv[y].T
    for copy in cp_x[1:5]:
        copy.wait_recv()
    for dy in (1, 3):
        xt[from_y(dy)] = x_recv[from_y(dy)].T
    fwds = [pass_on(1, 1), pass_on(2, 3)]
    for copy in cp_x[5:]:
        copy.wait_recv()
    xt[from_y(2)] = x_recv[from_y(2)].T
    cp_sib.wait_recv()
    acc[...] = dot(xt[y], g_all[y], ((1,), (0,)))
    fwds.append(pass_on(0, 2))
    for n, dy in enumerate((1, 3)):
        fwds[n].wait_recv()
        acc[...] += dot(xt[from_y(dy)], g_all[from_y(dy)], ((1,), (0,)))
    last_y = from_y(2)
    fwds[2].wait_recv()
    part_rows = PAIR * X
    slot = z * X + x
    for kz in range(Z // C):
        zz = c * (Z // C) + kz
        rows = pl.ds(kz * part_rows, part_rows)
        acc[rows, :] += dot(xt[last_y, rows, :], g_all[last_y], ((1,), (0,)))
        for kx in range(X):
            n = kz * X + kx
            at = pl.ds(n * PAIR, PAIR)
            rs_send[n] = jnp.concatenate([acc[at, pl.ds(0, HD)], acc[at, pl.ds(HD, HD)]], axis=0).astype(bf16)
        for kx in range(X):
            n = kz * X + kx
            is_self = (zz == z) & (kx == x)

            @pl.when(is_self)
            def _():
                pltpu.make_async_copy(rs_send.at[n], rs_recv.at[slot], rs_r.at[0]).start()

            @pl.when(jnp.logical_not(is_self))
            def _():
                send(rs_send.at[n], rs_recv.at[slot], rs_s.at[0], rs_r.at[0], place(y, zz, kx, c)).start()

    def rs_left():
        whole = Z // C * X

        @pl.when(taker)
        def _():
            part = pl.ds(0, whole - 1)
            send(rs_send.at[part], rs_recv.at[part], rs_s.at[0], rs_r.at[0], sib).wait_send()

        @pl.when(jnp.logical_not(taker))
        def _():
            part = pl.ds(0, whole)
            send(rs_send.at[part], rs_recv.at[part], rs_s.at[0], rs_r.at[0], sib).wait_send()

    late.append(rs_left)
    cp_w = send(wsum, wsum, w_s.at[0], w_r.at[0], sib)
    some_xy = pl.ds(1, Y * X - 1)
    all_xy = send(sq1.at[some_xy], sq1.at[some_xy], sq_s.at[0], sq_r.at[0], sib)
    some_zc = send(sq2.at[pl.ds(0, Z - 1)], sq2.at[pl.ds(0, Z - 1)], sq_s.at[1], sq_r.at[1], sib)
    all_zc = send(sq2, sq2, sq_s.at[1], sq_r.at[1], sib)

    def send_xy(i, _):
        to = place(lax.rem(y + i // X, Y), z, lax.rem(x + lax.rem(i, X), X), c)
        send(sq1.at[0], sq1.at[i], sq_s.at[0], sq_r.at[0], to).start()
        return 0

    def send_zc(i, _):
        to = place(y, lax.rem(z + Z // 2 + i // C, Z), x, lax.rem(c + 1 + lax.rem(i, C), C))

        @pl.when(i != Z + 1)
        def _():
            send(sq2.at[z], sq2.at[z], sq_s.at[1], sq_r.at[1], to).start()

        return 0

    @pl.when(taker)
    def _():
        send(rs_send, rs_recv, rs_s.at[0], rs_r.at[0], sib).wait_recv()
        total = rs_recv[0].astype(f32)
        for n in range(1, Z * X):
            total += rs_recv[n].astype(f32)
        wsum[...] = total
        cp_w.start()
        sq1[0] = jnp.broadcast_to(jnp.sum(total * total, axis=0, keepdims=True), (8, HD))
        lax.fori_loop(1, Y * X, send_xy, 0)
        all_xy.wait_recv()
        sq2[z] = jnp.sum(sq1[...], axis=0)
        lax.fori_loop(0, Z * C, send_zc, 0)
        some_zc.wait_recv()

    @pl.when(jnp.logical_not(taker))
    def _():
        cp_w.wait_recv()
        all_zc.wait_recv()

    def sums_left():
        @pl.when(taker)
        def _():
            cp_w.wait_send()
            all_xy.wait_send()
            for part in (pl.ds(0, Z), pl.ds(0, Z - 1)):
                send(sq2.at[part], sq2.at[part], sq_s.at[1], sq_r.at[1], sib).wait_send()

    late.append(sums_left)
    parts = []
    for k in range(C):
        at, then = pl.ds(k * ROWS, ROWS), pl.ds(PAIR + k * ROWS, ROWS)
        parts.append(jnp.concatenate([wsum[at, :], wsum[then, :]], axis=1))
    rows_sum = jnp.where(c == 0, parts[0], parts[1])

    lanes = jnp.sum(sq2[...], axis=0)
    square_total = jnp.sum(lanes[0:1], axis=1, keepdims=True)
    limit = math.sqrt(D * 2 * HD)
    clip = jnp.minimum(1.0, limit / (jnp.sqrt(square_total) + 1e-6))
    w_ref[...] = rows_sum * clip

    for copy in [cp_q, cp_do, cp_st, *cp_kv, *cp_x, *cp_ret, cp_dq, *cp_g, cp_sib, *fwds]:
        copy.wait_send()

    for wait in late:
        wait()


def on_device(queries, keys, values, attention_out, output_grad, log_norm, layer_input, doc_start, visible_blocks):
    hbm = pl.BlockSpec(memory_space=pl.ANY)
    dma = pltpu.SemaphoreType.DMA
    return pl.pallas_call(
        kernel,
        out_shape=(pltpu.VMEM((ROWS, 2 * HD), f32), pltpu.VMEM((T, HQ * HD), bf16)),
        in_specs=[hbm] * 9,
        out_specs=(pl.BlockSpec(memory_space=pltpu.VMEM),) * 2,
        scratch_shapes=[
            pltpu.VMEM((HQ, T), f32),
            pltpu.VMEM((1, T), jnp.int32),
            pltpu.VMEM((1, 5), jnp.int32),
            pltpu.VMEM((C, T, HQ * HD), bf16),
            pltpu.VMEM((C, T, HQ * HD), bf16),
            pltpu.VMEM((T, HQ * HD), bf16),
            pltpu.VMEM((3, T, HD), bf16),
            pltpu.VMEM((3, T, HD), bf16),
            pltpu.VMEM((C, 16, T), f32),
            pltpu.VMEM((HQ, 3 * T, 2 * T), bf16),
            pltpu.VMEM((2, T, 2 * HD), bf16),
            pltpu.VMEM((2, T, 2 * HD), bf16),
            pltpu.VMEM((C, T, HQ * HD), f32),
            pltpu.VMEM((T, HQ * HD), f32),
            pltpu.VMEM((Y, C * T, DC), bf16),
            pltpu.VMEM((Y, DC, C * T), bf16),
            pltpu.VMEM((Y, C * T, 2 * HD), bf16),
            pltpu.VMEM((DC, 2 * HD), f32),
            pltpu.VMEM((Z * X, 2 * PAIR, HD), bf16),
            pltpu.VMEM((Z * X, 2 * PAIR, HD), bf16),
            pltpu.VMEM((T, 2 * HD), f32),
            pltpu.VMEM((2 * PAIR, HD), f32),
            pltpu.VMEM((Y * X, 8, HD), f32),
            pltpu.VMEM((Z, 8, HD), f32),
            dma((9,)),
            dma((3,)),
            dma((3,)),
            dma((4,)),
            dma((4,)),
            dma((2,)),
            dma((2,)),
            dma((7,)),
            dma((7,)),
            dma((4,)),
            dma((4,)),
            dma((6,)),
            dma((1,)),
            dma((1,)),
            dma((1,)),
            dma((1,)),
            dma((1,)),
            dma((1,)),
            dma((2,)),
            dma((2,)),
        ],
        compiler_params=pltpu.CompilerParams(
            collective_id=0, has_side_effects=True, vmem_limit_bytes=56 * 2**20
        ),
        name="clip_attention_backward",
    )(
        queries,
        keys,
        values,
        attention_out,
        output_grad,
        log_norm,
        layer_input,
        doc_start.reshape(1, T),
        visible_blocks,
    )


def solution(mesh):
    both = ("inner", "outer")
    return jax.shard_map(
        on_device,
        mesh=mesh,
        in_specs=(
            P(both, None),
            P(both, None),
            P(both, None),
            P(both, None),
            P(both, None),
            P(None, both),
            P(both, None),
            P(both),
            P(both, None),
        ),
        out_specs=(P(both, None), P(both, None)),
        check_vma=False,
    )
```

```python
import math

import jax
import jax.numpy as jnp
from jax import lax
from jax.experimental import pallas as pl
from jax.experimental.pallas import tpu as pltpu
from jax.sharding import PartitionSpec as P

D = 5120
HD = 128
HQ = 5
T = 128
Y, Z, X, C = 4, 8, 4, 2
N = Y * Z * X * C
GROUP = 4
UNIT = D // GROUP
HALF = UNIT // C
ROWS = D // N
PAIR = C * ROWS
MSG = 48
FAR = 1.0e9
MESH = pl.DeviceIdType.MESH
f32, bf16 = jnp.float32, jnp.bfloat16
SCALE = 1.0 / math.sqrt(HD)
LOG2E = math.log2(math.e)


def place(y, z, x, c):
    return {"inner": y, "outer": (z * X + x) * C + c}


def dot(a, b, dims):
    return lax.dot_general(a, b, (dims, ((), ())), preferred_element_type=f32)


def kernel(
    q_hbm,
    k_hbm,
    v_hbm,
    o_hbm,
    do_hbm,
    lse_hbm,
    x_hbm,
    start_hbm,
    vis_hbm,
    w_ref,
    dq_ref,
    lse_ref,
    start_ref,
    vis_ref,
    q_all,
    do_all,
    o_own,
    kbuf,
    vbuf,
    stat,
    p_buf,
    ds_buf,
    ret_send,
    ret_recv,
    dq_part,
    dq_recv,
    x_recv,
    xt,
    own,
    g_all,
    acc,
    ex_send,
    ex_recv,
    rs_send,
    rs_recv,
    wsum,
    sq1,
    sq2,
    load_sem,
    qx_s,
    qx_r,
    kv_s,
    kv_r,
    ret_s,
    ret_r,
    x_s,
    x_r,
    g_s,
    g_r,
    dq_s,
    dq_r,
    ex_s,
    ex_r,
    rs_s,
    rs_r,
    w_s,
    w_r,
    sq_s,
    sq_r,
):
    y = lax.axis_index("inner")
    outer = lax.axis_index("outer")
    z = outer // (X * C)
    x = (outer // C) % X
    c = outer % C
    other = 1 - c
    block = y * (Z * X * C) + outer
    sib = place(y, z, x, other)
    taker = z // (Z // C) == c
    one = jnp.where(taker, 1, 0)
    ay, az = lax.rem(y, 2), lax.rem(z, 2)
    pair_y = lax.rem(y + jnp.where(ay == c, 1, Y - 1), Y)
    pair_z = lax.rem(z + jnp.where(az == c, 1, Z - 1), Z)
    peers = [(pair_y, z), (y, pair_z), (pair_y, pair_z)]

    def member(yy, zz):
        return 2 * lax.rem(yy, 2) + lax.rem(zz, 2)

    def unit_owner(yy, zz):
        return 1 - lax.rem(yy, 2) + 2 * lax.rem(zz, 2)

    me = member(y, z)

    def block_at(step):
        b = lax.rem(block + (step + N), N)
        return {"inner": b // (Z * X * C), "outer": lax.rem(b, Z * X * C)}

    def send(src, dst, ssem, rsem, device):
        copy = pltpu.make_async_remote_copy(
            src_ref=src, dst_ref=dst, send_sem=ssem, recv_sem=rsem, device_id=device, device_id_type=MESH
        )
        return copy

    late = []
    loads = [
        pltpu.make_async_copy(do_hbm, do_all.at[c], load_sem.at[0]),
        pltpu.make_async_copy(o_hbm, o_own, load_sem.at[1]),
        pltpu.make_async_copy(q_hbm, q_all.at[c], load_sem.at[2]),
        pltpu.make_async_copy(k_hbm, kbuf.at[0], load_sem.at[3]),
        pltpu.make_async_copy(v_hbm, vbuf.at[0], load_sem.at[4]),
        pltpu.make_async_copy(lse_hbm, lse_ref, load_sem.at[6]),
        pltpu.make_async_copy(start_hbm, start_ref, load_sem.at[7]),
        pltpu.make_async_copy(vis_hbm, vis_ref, load_sem.at[8]),
    ]
    for load in loads:
        load.start()

    barrier = pltpu.get_barrier_semaphore()

    def greet(device):
        pl.semaphore_signal(barrier, inc=1, device_id=device, device_id_type=MESH)

    def greet_sources(i, _):
        yy = 1 - ay + 2 * (i // (Z // 2 * X))
        zz = y // 2 + 2 * lax.rem(i // X, Z // 2)
        greet(place(yy, zz, lax.rem(i, X), c))
        return 0

    def greet_xy(i, _):
        greet(place(lax.rem(y + i // X, Y), z, lax.rem(x + lax.rem(i, X), X), c))
        return 0

    def greet_z(zz, _):
        cc = zz // (Z // C)

        @pl.when((zz != z) | (cc != c))
        def _():
            greet(place(y, zz, x, cc))

        return 0

    @pl.when(taker)
    def _():
        lax.fori_loop(0, Z * X, greet_sources, 0)

    lax.fori_loop(0, Z, greet_z, 0)

    @pl.when(taker)
    def _():
        lax.fori_loop(1, Y * X, greet_xy, 0)

    for step in (-4, 4, -2, 2):
        greet(block_at(step))
    for yy, zz in peers:
        greet(place(yy, zz, x, c))
    greet(sib)

    for i in (0, 1, 5, 6, 7):
        loads[i].wait()
    for h in range(HQ):
        cols = pl.ds(h * HD, HD)
        prod = do_all[c, :, cols].astype(f32) * o_own[:, cols].astype(f32)
        stat[c, pl.ds(h, 1), :] = jnp.sum(prod.T, axis=0, keepdims=True)
    stat[c, pl.ds(HQ, HQ), :] = lse_ref[...] * LOG2E
    first = start_ref[...].astype(f32)
    for d in range(5):
        kb = block - d
        wanted = jnp.where(kb >= 0, kb, -7)
        hit = jnp.max(jnp.where(vis_ref[...] == wanted, 1.0, 0.0), axis=1, keepdims=True)
        stat[c, pl.ds(10 + d, 1), :] = jnp.where(hit > 0.5, first, FAR)
    stat[c, pl.ds(15, 1), :] = jnp.full((1, T), FAR, f32)

    always = 1 + 4 + 3 + Z // C * X
    pl.semaphore_wait(barrier, always + one * (Y * X - 1 + Z * C - 1))

    cp_q = send(q_hbm, q_all.at[c], qx_s.at[0], qx_r.at[0], sib)
    cp_do = send(do_hbm, do_all.at[c], qx_s.at[1], qx_r.at[1], sib)
    cp_st = send(stat.at[c], stat.at[c], qx_s.at[2], qx_r.at[2], sib)
    cp_k, cp_v = [
        [send(src, buf.at[j], kv_s.at[2 * n + j - 1], kv_r.at[2 * n + j - 1], block_at(2 * j)) for j in (1, 2)]
        for n, (src, buf) in enumerate(((k_hbm, kbuf), (v_hbm, vbuf)))
    ]
    for copy in [*cp_k, cp_st, cp_q, cp_do, *cp_v]:
        copy.start()

    def x_cols(yy, zz):
        return x_hbm.at[:, pl.ds(pl.multiple_of(unit_owner(yy, zz) * UNIT, HD), UNIT)]

    x_own = pltpu.make_async_copy(x_cols(y, z), x_recv.at[me], load_sem.at[5])
    x_own.start()
    cp_x = []
    for i, (yy, zz) in enumerate(peers):
        copy = send(x_cols(yy, zz), x_recv.at[me], x_s.at[i], x_r.at[i], place(yy, zz, x, c))
        copy.start()
        cp_x.append(copy)

    for load in loads[2:5]:
        load.wait()
    cp_q.wait_recv()
    cp_do.wait_recv()
    cp_st.wait_recv()

    def row(r):
        return jnp.concatenate([stat[0, pl.ds(r, 1), :], stat[1, pl.ds(r, 1), :]], axis=1)

    iota_u = lax.broadcasted_iota(jnp.int32, (T, 2 * T), 0)
    iota_t = lax.broadcasted_iota(jnp.int32, (T, 2 * T), 1)
    pair_first = (block - c) * T
    query_pos = pair_first + iota_t

    def probs(j):
        key_pos = (block - 2 * j) * T + iota_u
        lows = []
        for i in range(C):
            d0, d1 = i + 2 * j, i - 1 + 2 * j
            at0, at1 = 10 + min(d0, 5), 10 + (d1 if d1 >= 0 else 5)
            lows.append(jnp.where(c == 0, stat[i, pl.ds(at0, 1), :], stat[i, pl.ds(at1, 1), :]))
        low = jnp.concatenate(lows, axis=1)
        allowed = (key_pos.astype(f32) >= low) & (key_pos <= query_pos)
        key_rows = kbuf[j]
        part = jnp.zeros((T, HD), f32)
        for h in range(HQ):
            cols = pl.ds(h * HD, HD)
            s = dot(key_rows, q_all[:, :, cols].reshape(2 * T, HD), ((1,), (1,)))
            prob = jnp.where(allowed, jnp.exp2(s * (SCALE * LOG2E) - row(HQ + h)), 0.0)
            p_buf[j, h] = prob
            part += dot(prob.astype(bf16), do_all[:, :, cols].reshape(2 * T, HD), ((1,), (0,)))
        return part

    def score_grads(j):
        value_rows = vbuf[j]
        part = jnp.zeros((T, HD), f32)
        for h in range(HQ):
            cols = pl.ds(h * HD, HD)
            dp = dot(value_rows, do_all[:, :, cols].reshape(2 * T, HD), ((1,), (1,)))
            ds = (p_buf[j, h] * (dp - row(h)) * SCALE).astype(bf16)
            ds_buf[h, pl.ds(j * T, T), :] = ds
            part += dot(ds, q_all[:, :, cols].reshape(2 * T, HD), ((1,), (0,)))
        return part

    def give_back(n, j, part):
        k = 2 * n + j - 1
        ret_send[k] = part.astype(bf16)
        copy = send(ret_send.at[k], ret_recv.at[k], ret_s.at[k], ret_r.at[k], block_at(-2 * j))
        copy.start()
        return copy

    cp_ret = []
    own[0] = probs(0)
    own[1] = score_grads(0)
    for j in (1, 2):
        cp_k[j - 1].wait_recv()
        cp_ret.append(give_back(0, j, probs(j)))
    for j in (1, 2):
        cp_v[j - 1].wait_recv()
        cp_ret.append(give_back(1, j, score_grads(j)))

    key_cat = kbuf[...].reshape(3 * T, HD)
    for h in range(HQ):
        part = dot(ds_buf[h], key_cat, ((0,), (0,)))
        dq_part[0, :, pl.ds(h * HD, HD)] = part[:T]
        dq_part[1, :, pl.ds(h * HD, HD)] = part[T:]
    cp_dq = send(dq_part.at[other], dq_recv, dq_s.at[0], dq_r.at[0], sib)
    cp_dq.start()

    x_own.wait()
    for copy in cp_x:
        copy.wait_recv()
    for m in range(GROUP):
        for hc in range(C):
            xt[hc, :, pl.ds(m * T, T)] = x_recv[m, :, pl.ds(hc * HALF, HALF)].T

    cp_g = []
    for n in range(2):
        cp_ret[2 * n].wait_recv()
        cp_ret[2 * n + 1].wait_recv()
        g_all[n, me] = (own[n] + ret_recv[2 * n].astype(f32) + ret_recv[2 * n + 1].astype(f32)).astype(bf16)
        mine = g_all.at[n, me]
        for i, (yy, zz) in reversed(list(enumerate(peers))):
            copy = send(mine, mine, g_s.at[n, i], g_r.at[n, i], place(yy, zz, x, c))
            copy.start()
            cp_g.append(copy)

    cp_dq.wait_recv()
    dq_ref[...] = (dq_part[c] + dq_recv[...]).astype(bf16)

    slot = (y // 2 * (Z // 2) + z // 2) * X + x
    to_y = unit_owner(y, z)
    part_rows = PAIR * X
    cp_ex = []
    for n in range(2):
        for copy in cp_g[3 * n : 3 * n + 3]:
            copy.wait_recv()
        grads = g_all[n].reshape(GROUP * T, HD)
        ex_send[n] = dot(xt[other], grads, ((1,), (0,))).astype(bf16)
        copy = send(ex_send.at[n], ex_recv.at[n], ex_s.at[n], ex_r.at[n], sib)
        copy.start()
        cp_ex.append(copy)
        acc[...] = dot(xt[c], grads, ((1,), (0,)))
        copy.wait_recv()
        for kz in range(Z // C):
            rows = pl.ds(kz * part_rows, part_rows)
            acc[rows, :] += ex_recv[n, rows, :].astype(f32)
            for kx in range(X):
                m = kz * X + kx
                part = jnp.concatenate([acc[pl.ds(m * PAIR, PAIR), :], jnp.zeros((MSG - PAIR, HD), f32)], axis=0)
                rs_send[n, m] = part.astype(bf16)
                send(
                    rs_send.at[n, m],
                    rs_recv.at[n, slot],
                    rs_s.at[n],
                    rs_r.at[n],
                    place(to_y, c * (Z // C) + kz, kx, c),
                ).start()

    def rs_left():
        for n in range(2):
            whole = rs_recv.at[n, pl.ds(0, Z // C * X)]
            send(rs_send.at[n], whole, rs_s.at[n], rs_r.at[n], sib).wait_send()

    late.append(rs_left)
    cp_w = send(wsum, wsum, w_s.at[0], w_r.at[0], sib)
    some_xy = pl.ds(1, Y * X - 1)
    all_xy = send(sq1.at[some_xy], sq1.at[some_xy], sq_s.at[0], sq_r.at[0], sib)
    some_zc = send(sq2.at[pl.ds(0, Z - 1)], sq2.at[pl.ds(0, Z - 1)], sq_s.at[1], sq_r.at[1], sib)
    all_zc = send(sq2, sq2, sq_s.at[1], sq_r.at[1], sib)

    def send_xy(i, _):
        to = place(lax.rem(y + i // X, Y), z, lax.rem(x + lax.rem(i, X), X), c)
        send(sq1.at[0], sq1.at[i], sq_s.at[0], sq_r.at[0], to).start()
        return 0

    def send_zc(i, _):
        to = place(y, lax.rem(z + Z // 2 + i // C, Z), x, lax.rem(c + 1 + lax.rem(i, C), C))

        @pl.when(i != Z + 1)
        def _():
            send(sq2.at[z], sq2.at[z], sq_s.at[1], sq_r.at[1], to).start()

        return 0

    @pl.when(taker)
    def _():
        squares = jnp.zeros((1, HD), f32)
        for n in range(2):
            send(rs_recv.at[n], rs_recv.at[n], rs_s.at[n], rs_r.at[n], sib).wait_recv()
            total = rs_recv[n, 0].astype(f32)
            for i in range(1, Z * X):
                total += rs_recv[n, i].astype(f32)
            wsum[n] = total
            squares += jnp.sum(total * total, axis=0, keepdims=True)
        cp_w.start()
        sq1[0] = squares
        lax.fori_loop(1, Y * X, send_xy, 0)
        all_xy.wait_recv()
        sq2[z] = jnp.sum(sq1[...], axis=0)
        lax.fori_loop(0, Z * C, send_zc, 0)
        some_zc.wait_recv()

    @pl.when(jnp.logical_not(taker))
    def _():
        cp_w.wait_recv()
        all_zc.wait_recv()

    def sums_left():
        @pl.when(taker)
        def _():
            cp_w.wait_send()
            all_xy.wait_send()
            for part in (pl.ds(0, Z), pl.ds(0, Z - 1)):
                send(sq2.at[part], sq2.at[part], sq_s.at[1], sq_r.at[1], sib).wait_send()

    late.append(sums_left)
    parts = []
    for k in range(C):
        at = pl.ds(k * ROWS, ROWS)
        parts.append(jnp.concatenate([wsum[1, at, :], wsum[0, at, :]], axis=1))
    rows_sum = jnp.where(c == 0, parts[0], parts[1])

    lanes = jnp.sum(sq2[...], axis=0)
    square_total = jnp.sum(lanes, axis=1, keepdims=True)
    limit = math.sqrt(D * 2 * HD)
    clip = jnp.minimum(1.0, limit / (jnp.sqrt(square_total) + 1e-6))
    w_ref[...] = rows_sum * clip

    for copy in [cp_q, cp_do, cp_st, *cp_k, *cp_v, *cp_x, *cp_ret, cp_dq, *cp_g, *cp_ex]:
        copy.wait_send()

    for wait in late:
        wait()


def on_device(queries, keys, values, attention_out, output_grad, log_norm, layer_input, doc_start, visible_blocks):
    hbm = pl.BlockSpec(memory_space=pl.ANY)
    dma = pltpu.SemaphoreType.DMA
    return pl.pallas_call(
        kernel,
        out_shape=(pltpu.VMEM((ROWS, 2 * HD), f32), pltpu.VMEM((T, HQ * HD), bf16)),
        in_specs=[hbm] * 9,
        out_specs=(pl.BlockSpec(memory_space=pltpu.VMEM),) * 2,
        scratch_shapes=[
            pltpu.VMEM((HQ, T), f32),
            pltpu.VMEM((1, T), jnp.int32),
            pltpu.VMEM((1, 5), jnp.int32),
            pltpu.VMEM((C, T, HQ * HD), bf16),
            pltpu.VMEM((C, T, HQ * HD), bf16),
            pltpu.VMEM((T, HQ * HD), bf16),
            pltpu.VMEM((3, T, HD), bf16),
            pltpu.VMEM((3, T, HD), bf16),
            pltpu.VMEM((C, 16, T), f32),
            pltpu.VMEM((3, HQ, T, 2 * T), f32),
            pltpu.VMEM((HQ, 3 * T, 2 * T), bf16),
            pltpu.VMEM((4, T, HD), bf16),
            pltpu.VMEM((4, T, HD), bf16),
            pltpu.VMEM((C, T, HQ * HD), f32),
            pltpu.VMEM((T, HQ * HD), f32),
            pltpu.VMEM((GROUP, T, UNIT), bf16),
            pltpu.VMEM((C, HALF, GROUP * T), bf16),
            pltpu.VMEM((2, T, HD), f32),
            pltpu.VMEM((2, GROUP, T, HD), bf16),
            pltpu.VMEM((HALF, HD), f32),
            pltpu.VMEM((2, HALF, HD), bf16),
            pltpu.VMEM((2, HALF, HD), bf16),
            pltpu.VMEM((2, Z // C * X, MSG, HD), bf16),
            pltpu.VMEM((2, Z * X, MSG, HD), bf16),
            pltpu.VMEM((2, MSG, HD), f32),
            pltpu.VMEM((Y * X, 1, HD), f32),
            pltpu.VMEM((Z, 1, HD), f32),
            dma((9,)),
            dma((3,)),
            dma((3,)),
            dma((4,)),
            dma((4,)),
            dma((4,)),
            dma((4,)),
            dma((3,)),
            dma((3,)),
            dma((2, 3)),
            dma((2, 3)),
            dma((1,)),
            dma((1,)),
            dma((2,)),
            dma((2,)),
            dma((2,)),
            dma((2,)),
            dma((1,)),
            dma((1,)),
            dma((2,)),
            dma((2,)),
        ],
        compiler_params=pltpu.CompilerParams(
            collective_id=0, has_side_effects=True, vmem_limit_bytes=56 * 2**20
        ),
        name="clip_attention_backward",
    )(
        queries,
        keys,
        values,
        attention_out,
        output_grad,
        log_norm,
        layer_input,
        doc_start.reshape(1, T),
        visible_blocks,
    )


def solution(mesh):
    both = ("inner", "outer")
    return jax.shard_map(
        on_device,
        mesh=mesh,
        in_specs=(
            P(both, None),
            P(both, None),
            P(both, None),
            P(both, None),
            P(both, None),
            P(None, both),
            P(both, None),
            P(both),
            P(both, None),
        ),
        out_specs=(P(both, None), P(both, None)),
        check_vma=False,
    )
```

```python
import math

import jax
import jax.numpy as jnp
from jax import lax
from jax.experimental import pallas as pl
from jax.experimental.pallas import tpu as pltpu
from jax.sharding import PartitionSpec as P

D = 5120
HD = 128
HQ = 5
T = 128
Y, Z, X, C = 4, 8, 4, 2
N = Y * Z * X * C
GROUP = 4
UNIT = D // GROUP
HALF = UNIT // C
ROWS = D // N
PAIR = C * ROWS
FAR = 1.0e9
MESH = pl.DeviceIdType.MESH
f32, bf16 = jnp.float32, jnp.bfloat16
SCALE = 1.0 / math.sqrt(HD)
LOG2E = math.log2(math.e)


def place(y, z, x, c):
    return {"inner": y, "outer": (z * X + x) * C + c}


def dot(a, b, dims):
    return lax.dot_general(a, b, (dims, ((), ())), preferred_element_type=f32)


def kernel(
    q_hbm,
    k_hbm,
    v_hbm,
    o_hbm,
    do_hbm,
    lse_hbm,
    x_hbm,
    start_hbm,
    vis_hbm,
    w_ref,
    dq_ref,
    lse_ref,
    start_ref,
    vis_ref,
    q_all,
    do_all,
    o_own,
    kbuf,
    vbuf,
    stat,
    p_buf,
    ds_buf,
    ret_send,
    ret_recv,
    dq_part,
    dq_recv,
    x_recv,
    xt,
    own,
    g_all,
    acc,
    ex_send,
    ex_recv,
    rs_send,
    rs_recv,
    wsum,
    sq1,
    sq2,
    load_sem,
    qx_s,
    qx_r,
    kv_s,
    kv_r,
    ret_s,
    ret_r,
    x_s,
    x_r,
    g_s,
    g_r,
    dq_s,
    dq_r,
    ex_s,
    ex_r,
    rs_s,
    rs_r,
    w_s,
    w_r,
    sq_s,
    sq_r,
    wave,
):
    y = lax.axis_index("inner")
    outer = lax.axis_index("outer")
    z = outer // (X * C)
    x = (outer // C) % X
    c = outer % C
    other = 1 - c
    block = y * (Z * X * C) + outer
    sib = place(y, z, x, other)
    taker = z // (Z // C) == c
    ay, az = lax.rem(y, 2), lax.rem(z, 2)
    pair_y = lax.rem(y + jnp.where(ay == c, 1, Y - 1), Y)
    pair_z = lax.rem(z + jnp.where(az == c, 1, Z - 1), Z)
    peers = [(pair_y, z), (y, pair_z), (pair_y, pair_z)]

    def member(yy, zz):
        return 2 * lax.rem(yy, 2) + lax.rem(zz, 2)

    def unit_owner(yy, zz):
        return 1 - lax.rem(yy, 2) + 2 * lax.rem(zz, 2)

    me = member(y, z)

    def block_at(step):
        b = lax.rem(block + (step + N), N)
        return {"inner": b // (Z * X * C), "outer": lax.rem(b, Z * X * C)}

    def send(src, dst, ssem, rsem, device):
        copy = pltpu.make_async_remote_copy(
            src_ref=src, dst_ref=dst, send_sem=ssem, recv_sem=rsem, device_id=device, device_id_type=MESH
        )
        return copy

    barrier = pltpu.get_barrier_semaphore()

    def greet(device):
        pl.semaphore_signal(barrier, inc=1, device_id=device, device_id_type=MESH)

    z_steps = [[place(y, lax.rem(z + dz, Z), x, c) for dz in dzs] for dzs in ((1, Z - 1), (2, Z - 2))]
    x_steps = [place(y, z, lax.rem(x + dx, X), c) for dx in range(1, X)]
    y_steps = [place(lax.rem(y + dy, Y), z, x, c) for dy in (1, Y - 1)]
    waves = [z_steps[0], z_steps[1], x_steps, y_steps]
    near = [sib, *[block_at(step) for step in (-4, 4, -2, 2)], *z_steps[0], *x_steps, *y_steps]
    near.append(place(pair_y, pair_z, x, c))
    for device in near:
        greet(device)

    def wave_out(k):
        for device in waves[k]:
            pl.semaphore_signal(wave.at[k], inc=1, device_id=device, device_id_type=MESH)

    def wave_in(k):
        pl.semaphore_wait(wave.at[k], len(waves[k]))

    late = []
    loads = [
        pltpu.make_async_copy(do_hbm, do_all.at[c], load_sem.at[0]),
        pltpu.make_async_copy(o_hbm, o_own, load_sem.at[1]),
        pltpu.make_async_copy(q_hbm, q_all.at[c], load_sem.at[2]),
        pltpu.make_async_copy(k_hbm, kbuf.at[0], load_sem.at[3]),
        pltpu.make_async_copy(v_hbm, vbuf.at[0], load_sem.at[4]),
        pltpu.make_async_copy(lse_hbm, lse_ref, load_sem.at[6]),
        pltpu.make_async_copy(start_hbm, start_ref, load_sem.at[7]),
        pltpu.make_async_copy(vis_hbm, vis_ref, load_sem.at[8]),
    ]
    for load in loads:
        load.start()

    pl.semaphore_wait(barrier, len(near))

    cp_q = send(q_hbm, q_all.at[c], qx_s.at[0], qx_r.at[0], sib)
    cp_do = send(do_hbm, do_all.at[c], qx_s.at[1], qx_r.at[1], sib)
    cp_st = send(stat.at[c], stat.at[c], qx_s.at[2], qx_r.at[2], sib)
    cp_k, cp_v = [
        [send(src, buf.at[j], kv_s.at[2 * n + j - 1], kv_r.at[2 * n + j - 1], block_at(2 * j)) for j in (1, 2)]
        for n, (src, buf) in enumerate(((k_hbm, kbuf), (v_hbm, vbuf)))
    ]
    for copy in [*cp_k, cp_q, cp_do, *cp_v]:
        copy.start()

    def x_cols(yy, zz):
        return x_hbm.at[:, pl.ds(pl.multiple_of(unit_owner(yy, zz) * UNIT, HD), UNIT)]

    x_own = pltpu.make_async_copy(x_cols(y, z), x_recv.at[me], load_sem.at[5])
    x_own.start()
    cp_x = []
    for i, (yy, zz) in enumerate(peers):
        copy = send(x_cols(yy, zz), x_recv.at[me], x_s.at[i], x_r.at[i], place(yy, zz, x, c))
        copy.start()
        cp_x.append(copy)

    for i in (0, 1, 5, 6, 7):
        loads[i].wait()
    for h in range(HQ):
        cols = pl.ds(h * HD, HD)
        prod = do_all[c, :, cols].astype(f32) * o_own[:, cols].astype(f32)
        stat[c, pl.ds(h, 1), :] = jnp.sum(prod.T, axis=0, keepdims=True)
    stat[c, pl.ds(HQ, HQ), :] = lse_ref[...] * LOG2E
    first = start_ref[...].astype(f32)
    for d in range(5):
        kb = block - d
        wanted = jnp.where(kb >= 0, kb, -7)
        hit = jnp.max(jnp.where(vis_ref[...] == wanted, 1.0, 0.0), axis=1, keepdims=True)
        stat[c, pl.ds(10 + d, 1), :] = jnp.where(hit > 0.5, first, FAR)
    stat[c, pl.ds(15, 1), :] = jnp.full((1, T), FAR, f32)
    cp_st.start()
    wave_out(0)

    for load in loads[2:5]:
        load.wait()
    cp_q.wait_recv()
    cp_do.wait_recv()
    cp_st.wait_recv()

    def row(r):
        return jnp.concatenate([stat[0, pl.ds(r, 1), :], stat[1, pl.ds(r, 1), :]], axis=1)

    iota_u = lax.broadcasted_iota(jnp.int32, (T, 2 * T), 0)
    iota_t = lax.broadcasted_iota(jnp.int32, (T, 2 * T), 1)
    pair_first = (block - c) * T
    query_pos = pair_first + iota_t

    def probs(j):
        key_pos = (block - 2 * j) * T + iota_u
        lows = []
        for i in range(C):
            d0, d1 = i + 2 * j, i - 1 + 2 * j
            at0, at1 = 10 + min(d0, 5), 10 + (d1 if d1 >= 0 else 5)
            lows.append(jnp.where(c == 0, stat[i, pl.ds(at0, 1), :], stat[i, pl.ds(at1, 1), :]))
        low = jnp.concatenate(lows, axis=1)
        allowed = (key_pos.astype(f32) >= low) & (key_pos <= query_pos)
        key_rows = kbuf[j]
        part = jnp.zeros((T, HD), f32)
        for h in range(HQ):
            cols = pl.ds(h * HD, HD)
            s = dot(key_rows, q_all[:, :, cols].reshape(2 * T, HD), ((1,), (1,)))
            prob = jnp.where(allowed, jnp.exp2(s * (SCALE * LOG2E) - row(HQ + h)), 0.0)
            p_buf[j, h] = prob
            part += dot(prob.astype(bf16), do_all[:, :, cols].reshape(2 * T, HD), ((1,), (0,)))
        return part

    def score_grads(j):
        value_rows = vbuf[j]
        part = jnp.zeros((T, HD), f32)
        for h in range(HQ):
            cols = pl.ds(h * HD, HD)
            dp = dot(value_rows, do_all[:, :, cols].reshape(2 * T, HD), ((1,), (1,)))
            ds = (p_buf[j, h] * (dp - row(h)) * SCALE).astype(bf16)
            ds_buf[h, pl.ds(j * T, T), :] = ds
            part += dot(ds, q_all[:, :, cols].reshape(2 * T, HD), ((1,), (0,)))
        return part

    def give_back(n, j, part):
        k = 2 * n + j - 1
        ret_send[k] = part.astype(bf16)
        copy = send(ret_send.at[k], ret_recv.at[k], ret_s.at[k], ret_r.at[k], block_at(-2 * j))
        copy.start()
        return copy

    cp_ret = []
    own[0] = probs(0)
    own[1] = score_grads(0)
    wave_in(0)
    wave_out(1)
    for j in (1, 2):
        cp_k[j - 1].wait_recv()
        cp_ret.append(give_back(0, j, probs(j)))
    for j in (1, 2):
        cp_v[j - 1].wait_recv()
        cp_ret.append(give_back(1, j, score_grads(j)))

    wave_in(1)
    wave_out(2)
    key_cat = kbuf[...].reshape(3 * T, HD)
    for h in range(HQ):
        part = dot(ds_buf[h], key_cat, ((0,), (0,)))
        dq_part[0, :, pl.ds(h * HD, HD)] = part[:T]
        dq_part[1, :, pl.ds(h * HD, HD)] = part[T:]
    cp_dq = send(dq_part.at[other], dq_recv, dq_s.at[0], dq_r.at[0], sib)
    cp_dq.start()

    wave_in(2)
    wave_out(3)
    x_own.wait()
    for copy in cp_x:
        copy.wait_recv()
    for m in range(GROUP):
        for hc in range(C):
            xt[hc, :, pl.ds(m * T, T)] = x_recv[m, :, pl.ds(hc * HALF, HALF)].T

    cp_g = []
    for n in range(2):
        cp_ret[2 * n].wait_recv()
        cp_ret[2 * n + 1].wait_recv()
        g_all[n, me] = (own[n] + ret_recv[2 * n].astype(f32) + ret_recv[2 * n + 1].astype(f32)).astype(bf16)
        mine = g_all.at[n, me]
        for i, (yy, zz) in reversed(list(enumerate(peers))):
            copy = send(mine, mine, g_s.at[n, i], g_r.at[n, i], place(yy, zz, x, c))
            copy.start()
            cp_g.append(copy)

    cp_dq.wait_recv()
    dq_ref[...] = (dq_part[c] + dq_recv[...]).astype(bf16)

    for copy in cp_g:
        copy.wait_recv()
    grads = jnp.concatenate([g_all[1].reshape(GROUP * T, HD), g_all[0].reshape(GROUP * T, HD)], axis=1)
    part_rows = PAIR * X
    cp_ex = []
    for kz in range(Z // C):
        ex_send[kz] = dot(xt[other, pl.ds(kz * part_rows, part_rows), :], grads, ((1,), (0,))).astype(bf16)
        copy = send(ex_send.at[kz], ex_recv.at[kz], ex_s.at[kz], ex_r.at[kz], sib)
        copy.start()
        cp_ex.append(copy)
    for kz in range(Z // C):
        acc[kz] = dot(xt[c, pl.ds(kz * part_rows, part_rows), :], grads, ((1,), (0,)))
    wave_in(3)
    slot = (y // 2 * (Z // 2) + z // 2) * X + x
    to_y = unit_owner(y, z)
    for kz in range(Z // C):
        cp_ex[kz].wait_recv()
        acc[kz] += ex_recv[kz].astype(f32)
        for kx in range(X):
            at = pl.ds(kx * PAIR, PAIR)
            part = jnp.concatenate([acc[kz, at, pl.ds(0, HD)], acc[kz, at, pl.ds(HD, HD)]], axis=0)
            m = kz * X + kx
            rs_send[m] = part.astype(bf16)
            to = place(to_y, c * (Z // C) + kz, kx, c)
            send(rs_send.at[m], rs_recv.at[slot], rs_s.at[0], rs_r.at[0], to).start()

    def rs_left():
        whole = rs_recv.at[pl.ds(0, Z // C * X)]
        send(rs_send, whole, rs_s.at[0], rs_r.at[0], sib).wait_send()

    late.append(rs_left)
    cp_w = send(wsum, wsum, w_s.at[0], w_r.at[0], sib)
    some_xy = pl.ds(1, Y * X - 1)
    all_xy = send(sq1.at[some_xy], sq1.at[some_xy], sq_s.at[0], sq_r.at[0], sib)
    some_zc = send(sq2.at[pl.ds(0, Z - 1)], sq2.at[pl.ds(0, Z - 1)], sq_s.at[1], sq_r.at[1], sib)
    all_zc = send(sq2, sq2, sq_s.at[1], sq_r.at[1], sib)

    def send_xy(i, _):
        to = place(lax.rem(y + i // X, Y), z, lax.rem(x + lax.rem(i, X), X), c)
        send(sq1.at[0], sq1.at[i], sq_s.at[0], sq_r.at[0], to).start()
        return 0

    def send_zc(i, _):
        to = place(y, lax.rem(z + Z // 2 + i // C, Z), x, lax.rem(c + 1 + lax.rem(i, C), C))

        @pl.when(i != Z + 1)
        def _():
            send(sq2.at[z], sq2.at[z], sq_s.at[1], sq_r.at[1], to).start()

        return 0

    @pl.when(taker)
    def _():
        send(rs_recv, rs_recv, rs_s.at[0], rs_r.at[0], sib).wait_recv()
        total = rs_recv[0].astype(f32)
        for i in range(1, Z * X):
            total += rs_recv[i].astype(f32)
        wsum[...] = total
        cp_w.start()
        sq1[0] = jnp.sum(total * total, axis=0, keepdims=True)
        lax.fori_loop(1, Y * X, send_xy, 0)
        all_xy.wait_recv()
        sq2[z] = jnp.sum(sq1[...], axis=0)
        lax.fori_loop(0, Z * C, send_zc, 0)
        some_zc.wait_recv()

    @pl.when(jnp.logical_not(taker))
    def _():
        cp_w.wait_recv()
        all_zc.wait_recv()

    def sums_left():
        @pl.when(taker)
        def _():
            cp_w.wait_send()
            all_xy.wait_send()
            for part in (pl.ds(0, Z), pl.ds(0, Z - 1)):
                send(sq2.at[part], sq2.at[part], sq_s.at[1], sq_r.at[1], sib).wait_send()

    late.append(sums_left)
    parts = []
    for k in range(C):
        at, then = pl.ds(k * ROWS, ROWS), pl.ds(PAIR + k * ROWS, ROWS)
        parts.append(jnp.concatenate([wsum[at, :], wsum[then, :]], axis=1))
    rows_sum = jnp.where(c == 0, parts[0], parts[1])

    lanes = jnp.sum(sq2[...], axis=0)
    square_total = jnp.sum(lanes, axis=1, keepdims=True)
    limit = math.sqrt(D * 2 * HD)
    clip = jnp.minimum(1.0, limit / (jnp.sqrt(square_total) + 1e-6))
    w_ref[...] = rows_sum * clip

    for copy in [cp_q, cp_do, cp_st, *cp_k, *cp_v, *cp_x, *cp_ret, cp_dq, *cp_g, *cp_ex]:
        copy.wait_send()

    for wait in late:
        wait()


def on_device(queries, keys, values, attention_out, output_grad, log_norm, layer_input, doc_start, visible_blocks):
    hbm = pl.BlockSpec(memory_space=pl.ANY)
    dma = pltpu.SemaphoreType.DMA
    return pl.pallas_call(
        kernel,
        out_shape=(pltpu.VMEM((ROWS, 2 * HD), f32), pltpu.VMEM((T, HQ * HD), bf16)),
        in_specs=[hbm] * 9,
        out_specs=(pl.BlockSpec(memory_space=pltpu.VMEM),) * 2,
        scratch_shapes=[
            pltpu.VMEM((HQ, T), f32),
            pltpu.VMEM((1, T), jnp.int32),
            pltpu.VMEM((1, 5), jnp.int32),
            pltpu.VMEM((C, T, HQ * HD), bf16),
            pltpu.VMEM((C, T, HQ * HD), bf16),
            pltpu.VMEM((T, HQ * HD), bf16),
            pltpu.VMEM((3, T, HD), bf16),
            pltpu.VMEM((3, T, HD), bf16),
            pltpu.VMEM((C, 16, T), f32),
            pltpu.VMEM((3, HQ, T, 2 * T), f32),
            pltpu.VMEM((HQ, 3 * T, 2 * T), bf16),
            pltpu.VMEM((4, T, HD), bf16),
            pltpu.VMEM((4, T, HD), bf16),
            pltpu.VMEM((C, T, HQ * HD), f32),
            pltpu.VMEM((T, HQ * HD), f32),
            pltpu.VMEM((GROUP, T, UNIT), bf16),
            pltpu.VMEM((C, HALF, GROUP * T), bf16),
            pltpu.VMEM((2, T, HD), f32),
            pltpu.VMEM((2, GROUP, T, HD), bf16),
            pltpu.VMEM((Z // C, PAIR * X, 2 * HD), f32),
            pltpu.VMEM((Z // C, PAIR * X, 2 * HD), bf16),
            pltpu.VMEM((Z // C, PAIR * X, 2 * HD), bf16),
            pltpu.VMEM((Z // C * X, 2 * PAIR, HD), bf16),
            pltpu.VMEM((Z * X, 2 * PAIR, HD), bf16),
            pltpu.VMEM((2 * PAIR, HD), f32),
            pltpu.VMEM((Y * X, 1, HD), f32),
            pltpu.VMEM((Z, 1, HD), f32),
            dma((9,)),
            dma((3,)),
            dma((3,)),
            dma((4,)),
            dma((4,)),
            dma((4,)),
            dma((4,)),
            dma((3,)),
            dma((3,)),
            dma((2, 3)),
            dma((2, 3)),
            dma((1,)),
            dma((1,)),
            dma((Z // C,)),
            dma((Z // C,)),
            dma((1,)),
            dma((1,)),
            dma((1,)),
            dma((1,)),
            dma((2,)),
            dma((2,)),
            pltpu.SemaphoreType.REGULAR((4,)),
        ],
        compiler_params=pltpu.CompilerParams(
            collective_id=0, has_side_effects=True, vmem_limit_bytes=56 * 2**20
        ),
        name="clip_attention_backward",
    )(
        queries,
        keys,
        values,
        attention_out,
        output_grad,
        log_norm,
        layer_input,
        doc_start.reshape(1, T),
        visible_blocks,
    )


def solution(mesh):
    both = ("inner", "outer")
    return jax.shard_map(
        on_device,
        mesh=mesh,
        in_specs=(
            P(both, None),
            P(both, None),
            P(both, None),
            P(both, None),
            P(both, None),
            P(None, both),
            P(both, None),
            P(both),
            P(both, None),
        ),
        out_specs=(P(both, None), P(both, None)),
        check_vma=False,
    )
```

```python
import math

import jax
import jax.numpy as jnp
from jax import lax
from jax.experimental import pallas as pl
from jax.experimental.pallas import tpu as pltpu
from jax.sharding import PartitionSpec as P

D = 5120
HD = 128
HQ = 5
T = 128
Y, Z, X, C = 4, 8, 4, 2
N = Y * Z * X * C
GROUP = 4
UNIT = D // GROUP
HALF = UNIT // C
ROWS = D // N
PAIR = C * ROWS
EARLY = 32
FAR = 1.0e9
MESH = pl.DeviceIdType.MESH
f32, bf16 = jnp.float32, jnp.bfloat16
SCALE = 1.0 / math.sqrt(HD)
LOG2E = math.log2(math.e)


def place(y, z, x, c):
    return {"inner": y, "outer": (z * X + x) * C + c}


def dot(a, b, dims):
    return lax.dot_general(a, b, (dims, ((), ())), preferred_element_type=f32)


def kernel(
    q_hbm,
    k_hbm,
    v_hbm,
    o_hbm,
    do_hbm,
    lse_hbm,
    x_hbm,
    start_hbm,
    vis_hbm,
    w_ref,
    dq_ref,
    lse_ref,
    start_ref,
    vis_ref,
    q_all,
    do_all,
    o_own,
    kbuf,
    vbuf,
    stat,
    p_buf,
    p_half,
    ds_buf,
    ret_send,
    ret_recv,
    dq_part,
    dq_recv,
    x_recv,
    xt,
    own,
    g_all,
    acc,
    ex_send,
    ex_recv,
    rs_send,
    rs_recv,
    wsum,
    sq1,
    sq2,
    load_sem,
    qx_s,
    qx_r,
    kv_s,
    kv_r,
    ret_s,
    ret_r,
    x_s,
    x_r,
    g_s,
    g_r,
    dq_s,
    dq_r,
    ex_s,
    ex_r,
    rs_s,
    rs_r,
    w_s,
    w_r,
    sq_s,
    sq_r,
    wave,
):
    y = lax.axis_index("inner")
    outer = lax.axis_index("outer")
    z = outer // (X * C)
    x = (outer // C) % X
    c = outer % C
    other = 1 - c
    block = y * (Z * X * C) + outer
    sib = place(y, z, x, other)
    taker = z // (Z // C) == c
    dz = jnp.where(c == 0, 1, Z - 1)
    peers = [(lax.rem(y + 1, Y), z), (lax.rem(y + Y - 1, Y), z), (y, lax.rem(z + dz, Z))]

    def unit_owner(yy, zz):
        return lax.rem(yy + 2 * zz + 1, Y)

    def block_at(step):
        b = lax.rem(block + (step + N), N)
        return {"inner": b // (Z * X * C), "outer": lax.rem(b, Z * X * C)}

    def send(src, dst, ssem, rsem, device):
        copy = pltpu.make_async_remote_copy(
            src_ref=src, dst_ref=dst, send_sem=ssem, recv_sem=rsem, device_id=device, device_id_type=MESH
        )
        return copy

    barrier = pltpu.get_barrier_semaphore()

    def greet(device):
        pl.semaphore_signal(barrier, inc=1, device_id=device, device_id_type=MESH)

    z_steps = [[place(y, lax.rem(z + dz, Z), x, c) for dz in dzs] for dzs in ((1, Z - 1), (2, Z - 2))]
    x_steps = [place(y, z, lax.rem(x + dx, X), c) for dx in range(1, X)]
    y_steps = [place(lax.rem(y + dy, Y), z, x, c) for dy in (1, Y - 1)]
    waves = [z_steps[0], z_steps[1], x_steps, y_steps]
    near = [sib, *[block_at(step) for step in (-4, 4, -2, 2)], *z_steps[0], *x_steps, *y_steps]
    for device in near:
        greet(device)

    def wave_out(k):
        for device in waves[k]:
            pl.semaphore_signal(wave.at[k], inc=1, device_id=device, device_id_type=MESH)

    def wave_in(k):
        pl.semaphore_wait(wave.at[k], len(waves[k]))

    late = []
    loads = [
        pltpu.make_async_copy(do_hbm, do_all.at[c], load_sem.at[0]),
        pltpu.make_async_copy(o_hbm, o_own, load_sem.at[1]),
        pltpu.make_async_copy(q_hbm, q_all.at[c], load_sem.at[2]),
        pltpu.make_async_copy(k_hbm, kbuf.at[0], load_sem.at[3]),
        pltpu.make_async_copy(v_hbm, vbuf.at[0], load_sem.at[4]),
        pltpu.make_async_copy(lse_hbm, lse_ref, load_sem.at[6]),
        pltpu.make_async_copy(start_hbm, start_ref, load_sem.at[7]),
        pltpu.make_async_copy(vis_hbm, vis_ref, load_sem.at[8]),
    ]
    for load in loads:
        load.start()

    pl.semaphore_wait(barrier, len(near))

    cp_q = send(q_hbm, q_all.at[c], qx_s.at[0], qx_r.at[0], sib)
    cp_do = send(do_hbm, do_all.at[c], qx_s.at[1], qx_r.at[1], sib)
    cp_st = send(stat.at[c], stat.at[c], qx_s.at[2], qx_r.at[2], sib)
    cp_k, cp_v = [
        [send(src, buf.at[j], kv_s.at[2 * n + j - 1], kv_r.at[2 * n + j - 1], block_at(2 * j)) for j in (1, 2)]
        for n, (src, buf) in enumerate(((k_hbm, kbuf), (v_hbm, vbuf)))
    ]
    for copy in [*cp_k, cp_q, cp_do, *cp_v]:
        copy.start()

    def x_cols(yy, zz):
        return x_hbm.at[:, pl.ds(pl.multiple_of(unit_owner(yy, zz) * UNIT, HD), UNIT)]

    x_own = pltpu.make_async_copy(x_cols(y, z), x_recv.at[0], load_sem.at[5])
    x_own.start()
    cp_x = []
    for i, (yy, zz) in enumerate(peers):
        copy = send(x_cols(yy, zz), x_recv.at[1 + i], x_s.at[i], x_r.at[i], place(yy, zz, x, c))
        copy.start()
        cp_x.append(copy)

    for i in (0, 1, 5, 6, 7):
        loads[i].wait()
    for h in range(HQ):
        cols = pl.ds(h * HD, HD)
        prod = do_all[c, :, cols].astype(f32) * o_own[:, cols].astype(f32)
        stat[c, pl.ds(h, 1), :] = jnp.sum(prod.T, axis=0, keepdims=True)
    stat[c, pl.ds(HQ, HQ), :] = lse_ref[...] * LOG2E
    first = start_ref[...].astype(f32)
    for d in range(5):
        kb = block - d
        wanted = jnp.where(kb >= 0, kb, -7)
        hit = jnp.max(jnp.where(vis_ref[...] == wanted, 1.0, 0.0), axis=1, keepdims=True)
        stat[c, pl.ds(10 + d, 1), :] = jnp.where(hit > 0.5, first, FAR)
    stat[c, pl.ds(15, 1), :] = jnp.full((1, T), FAR, f32)
    cp_st.start()
    wave_out(0)

    for load in loads[2:5]:
        load.wait()
    cp_q.wait_recv()
    cp_do.wait_recv()
    cp_st.wait_recv()

    def row(r):
        return jnp.concatenate([stat[0, pl.ds(r, 1), :], stat[1, pl.ds(r, 1), :]], axis=1)


    def lowest(j):
        lows = []
        for i in range(C):
            d0, d1 = i + 2 * j, i - 1 + 2 * j
            at0, at1 = 10 + min(d0, 5), 10 + (d1 if d1 >= 0 else 5)
            lows.append(jnp.where(c == 0, stat[i, pl.ds(at0, 1), :], stat[i, pl.ds(at1, 1), :]))
        return jnp.concatenate(lows, axis=1)

    def heads(ref, h):
        return ref[:, :, pl.ds(h * HD, HD)].reshape(2 * T, HD)

    def probs(first, count):
        rows = pl.ds(first * T, count * T)
        iota_u = lax.broadcasted_iota(jnp.int32, (count * T, 2 * T), 0)
        iota_t = lax.broadcasted_iota(jnp.int32, (count * T, 2 * T), 1)
        key_pos = (block - 2 * first) * T + iota_u
        low = lowest(first)
        if count == 2:
            key_pos = jnp.where(iota_u < T, key_pos, key_pos - 3 * T)
            low = jnp.where(iota_u < T, low, lowest(first + 1))
        allowed = (key_pos.astype(f32) >= low) & (key_pos <= (block - c) * T + iota_t)
        key_rows = kbuf[first : first + count].reshape(count * T, HD)
        for h in range(HQ):
            s = dot(key_rows, heads(q_all, h), ((1,), (1,)))
            prob = jnp.where(allowed, jnp.exp2(s * (SCALE * LOG2E) - row(HQ + h)), 0.0)
            p_buf[h, rows, :] = prob
            p_half[h, rows, :] = prob.astype(bf16)
        part = jnp.zeros((count * T, HD), f32)
        for h in range(HQ):
            part += dot(p_half[h, rows, :], heads(do_all, h), ((1,), (0,)))
        return part

    def score_grads(first, count):
        rows = pl.ds(first * T, count * T)
        value_rows = vbuf[first : first + count].reshape(count * T, HD)
        for h in range(HQ):
            dp = dot(value_rows, heads(do_all, h), ((1,), (1,)))
            ds_buf[h, rows, :] = (p_buf[h, rows, :] * (dp - row(h)) * SCALE).astype(bf16)
        part = jnp.zeros((count * T, HD), f32)
        for h in range(HQ):
            part += dot(ds_buf[h, rows, :], heads(q_all, h), ((1,), (0,)))
        return part

    def give_back(n, part):
        for j in (2, 1):
            k = 2 * n + j - 1
            ret_send[k] = part[(j - 1) * T : j * T].astype(bf16)
            copy = send(ret_send.at[k], ret_recv.at[k], ret_s.at[k], ret_r.at[k], block_at(-2 * j))
            copy.start()
            cp_ret.append(copy)

    cp_ret = []
    own[0] = probs(0, 1)
    own[1] = score_grads(0, 1)
    wave_in(0)
    wave_out(1)
    for copy in cp_k:
        copy.wait_recv()
    give_back(0, probs(1, 2))
    for copy in cp_v:
        copy.wait_recv()
    give_back(1, score_grads(1, 2))

    wave_in(1)
    wave_out(2)
    key_cat = kbuf[...].reshape(3 * T, HD)
    for h in range(HQ):
        part = dot(ds_buf[h], key_cat, ((0,), (0,)))
        dq_part[0, :, pl.ds(h * HD, HD)] = part[:T]
        dq_part[1, :, pl.ds(h * HD, HD)] = part[T:]
    cp_dq = send(dq_part.at[other], dq_recv, dq_s.at[0], dq_r.at[0], sib)
    cp_dq.start()

    def transpose(m):
        for hc in range(C):
            xt[hc, m] = x_recv[m, :, pl.ds(hc * HALF, HALF)].T

    x_own.wait()
    transpose(0)

    cp_g = []
    for n in range(2):
        cp_ret[2 * n].wait_recv()
        cp_ret[2 * n + 1].wait_recv()
        g_all[n, 0] = (own[n] + ret_recv[2 * n].astype(f32) + ret_recv[2 * n + 1].astype(f32)).astype(bf16)
        for i, (yy, zz) in enumerate(peers):
            copy = send(g_all.at[n, 0], g_all.at[n, 1 + i], g_s.at[n, i], g_r.at[n, i], place(yy, zz, x, c))
            copy.start()
            cp_g.append(copy)
        if n == 0:
            wave_in(2)
            wave_out(3)
            cp_dq.wait_recv()
            dq_ref[...] = (dq_part[c] + dq_recv[...]).astype(bf16)

    for i in range(GROUP - 1):
        cp_x[i].wait_recv()
        transpose(1 + i)

    slot = z * X + x
    to_y = unit_owner(y, z)
    parts = 2
    step = HALF // parts
    cp_ex = []

    def product(hc, n, rows):
        total = dot(xt[hc, 0, rows, :], g_all[n, 0], ((1,), (0,)))
        for m in range(1, GROUP):
            total += dot(xt[hc, m, rows, :], g_all[n, m], ((1,), (0,)))
        return total

    for n in range(2):
        for copy in cp_g[3 * n : 3 * n + 3]:
            copy.wait_recv()
        for p in range(parts):
            ex_send[n, p] = product(other, n, pl.ds(p * step, step)).astype(bf16)
            copy = send(ex_send.at[n, p], ex_recv.at[n, p], ex_s.at[n, p], ex_r.at[n, p], sib)
            copy.start()
            cp_ex.append(copy)
        for p in range(parts):
            acc[n, pl.ds(p * step, step), :] = product(c, n, pl.ds(p * step, step))
        if n == 0:
            wave_in(3)
        for p in range(parts):
            cp_ex[parts * n + p].wait_recv()
            acc[n, pl.ds(p * step, step), :] += ex_recv[n, p].astype(f32)
            for i in range(step // PAIR):
                m = p * (step // PAIR) + i
                if n == 0:
                    rows = pl.ds(0, EARLY)
                    rs_send[m, rows, :] = acc[0, pl.ds(m * PAIR, EARLY), :].astype(bf16)
                else:
                    rows = pl.ds(EARLY, 2 * PAIR - EARLY)
                    left = acc[0, pl.ds(m * PAIR + EARLY, PAIR - EARLY), :]
                    both = jnp.concatenate([left, acc[1, pl.ds(m * PAIR, PAIR), :]], axis=0)
                    rs_send[m, rows, :] = both.astype(bf16)
                to = place(to_y, c * (Z // C) + m // X, m % X, c)
                send(rs_send.at[m, rows], rs_recv.at[slot, rows], rs_s.at[n], rs_r.at[n], to).start()

    shares = (pl.ds(0, EARLY), pl.ds(EARLY, 2 * PAIR - EARLY))

    def rs_left():
        for n, rows in enumerate(shares):
            some = rs_recv.at[pl.ds(0, Z // C * X), rows]
            send(rs_send.at[:, rows], some, rs_s.at[n], rs_r.at[n], sib).wait_send()

    late.append(rs_left)
    cp_w = send(wsum, wsum, w_s.at[0], w_r.at[0], sib)
    some_xy = pl.ds(1, Y * X - 1)
    all_xy = send(sq1.at[some_xy], sq1.at[some_xy], sq_s.at[0], sq_r.at[0], sib)
    some_zc = send(sq2.at[pl.ds(0, Z - 1)], sq2.at[pl.ds(0, Z - 1)], sq_s.at[1], sq_r.at[1], sib)
    all_zc = send(sq2, sq2, sq_s.at[1], sq_r.at[1], sib)

    def send_xy(i, _):
        to = place(lax.rem(y + i // X, Y), z, lax.rem(x + lax.rem(i, X), X), c)
        send(sq1.at[0], sq1.at[i], sq_s.at[0], sq_r.at[0], to).start()
        return 0

    def send_zc(i, _):
        to = place(y, lax.rem(z + Z // 2 + i // C, Z), x, lax.rem(c + 1 + lax.rem(i, C), C))

        @pl.when(i != Z + 1)
        def _():
            send(sq2.at[z], sq2.at[z], sq_s.at[1], sq_r.at[1], to).start()

        return 0

    @pl.when(taker)
    def _():
        squares = jnp.zeros((1, HD), f32)
        for n, rows in enumerate(shares):
            here = rs_recv.at[:, rows]
            send(here, here, rs_s.at[n], rs_r.at[n], sib).wait_recv()
            total = rs_recv[0, rows, :].astype(f32)
            for i in range(1, Z * X):
                total += rs_recv[i, rows, :].astype(f32)
            wsum[rows, :] = total
            squares += jnp.sum(total * total, axis=0, keepdims=True)
        cp_w.start()
        sq1[0] = squares
        lax.fori_loop(1, Y * X, send_xy, 0)
        all_xy.wait_recv()
        sq2[z] = jnp.sum(sq1[...], axis=0)
        lax.fori_loop(0, Z * C, send_zc, 0)
        some_zc.wait_recv()

    @pl.when(jnp.logical_not(taker))
    def _():
        cp_w.wait_recv()
        all_zc.wait_recv()

    def sums_left():
        @pl.when(taker)
        def _():
            cp_w.wait_send()
            all_xy.wait_send()
            for part in (pl.ds(0, Z), pl.ds(0, Z - 1)):
                send(sq2.at[part], sq2.at[part], sq_s.at[1], sq_r.at[1], sib).wait_send()

    late.append(sums_left)
    halves = []
    for k in range(C):
        at, then = pl.ds(k * ROWS, ROWS), pl.ds(PAIR + k * ROWS, ROWS)
        halves.append(jnp.concatenate([wsum[then, :], wsum[at, :]], axis=1))
    rows_sum = jnp.where(c == 0, halves[0], halves[1])

    lanes = jnp.sum(sq2[...], axis=0)
    square_total = jnp.sum(lanes, axis=1, keepdims=True)
    limit = math.sqrt(D * 2 * HD)
    clip = jnp.minimum(1.0, limit / (jnp.sqrt(square_total) + 1e-6))
    w_ref[...] = rows_sum * clip

    for copy in [cp_q, cp_do, cp_st, *cp_k, *cp_v, *cp_x, *cp_ret, cp_dq, *cp_g, *cp_ex]:
        copy.wait_send()

    for wait in late:
        wait()


def on_device(queries, keys, values, attention_out, output_grad, log_norm, layer_input, doc_start, visible_blocks):
    hbm = pl.BlockSpec(memory_space=pl.ANY)
    dma = pltpu.SemaphoreType.DMA
    return pl.pallas_call(
        kernel,
        out_shape=(pltpu.VMEM((ROWS, 2 * HD), f32), pltpu.VMEM((T, HQ * HD), bf16)),
        in_specs=[hbm] * 9,
        out_specs=(pl.BlockSpec(memory_space=pltpu.VMEM),) * 2,
        scratch_shapes=[
            pltpu.VMEM((HQ, T), f32),
            pltpu.VMEM((1, T), jnp.int32),
            pltpu.VMEM((1, 5), jnp.int32),
            pltpu.VMEM((C, T, HQ * HD), bf16),
            pltpu.VMEM((C, T, HQ * HD), bf16),
            pltpu.VMEM((T, HQ * HD), bf16),
            pltpu.VMEM((3, T, HD), bf16),
            pltpu.VMEM((3, T, HD), bf16),
            pltpu.VMEM((C, 16, T), f32),
            pltpu.VMEM((HQ, 3 * T, 2 * T), f32),
            pltpu.VMEM((HQ, 3 * T, 2 * T), bf16),
            pltpu.VMEM((HQ, 3 * T, 2 * T), bf16),
            pltpu.VMEM((4, T, HD), bf16),
            pltpu.VMEM((4, T, HD), bf16),
            pltpu.VMEM((C, T, HQ * HD), f32),
            pltpu.VMEM((T, HQ * HD), f32),
            pltpu.VMEM((GROUP, T, UNIT), bf16),
            pltpu.VMEM((C, GROUP, HALF, T), bf16),
            pltpu.VMEM((2, T, HD), f32),
            pltpu.VMEM((2, GROUP, T, HD), bf16),
            pltpu.VMEM((2, HALF, HD), f32),
            pltpu.VMEM((2, 2, HALF // 2, HD), bf16),
            pltpu.VMEM((2, 2, HALF // 2, HD), bf16),
            pltpu.VMEM((Z // C * X, 2 * PAIR, HD), bf16),
            pltpu.VMEM((Z * X, 2 * PAIR, HD), bf16),
            pltpu.VMEM((2 * PAIR, HD), f32),
            pltpu.VMEM((Y * X, 1, HD), f32),
            pltpu.VMEM((Z, 1, HD), f32),
            dma((9,)),
            dma((3,)),
            dma((3,)),
            dma((4,)),
            dma((4,)),
            dma((4,)),
            dma((4,)),
            dma((3,)),
            dma((3,)),
            dma((2, 3)),
            dma((2, 3)),
            dma((1,)),
            dma((1,)),
            dma((2, 2)),
            dma((2, 2)),
            dma((2,)),
            dma((2,)),
            dma((1,)),
            dma((1,)),
            dma((2,)),
            dma((2,)),
            pltpu.SemaphoreType.REGULAR((4,)),
        ],
        compiler_params=pltpu.CompilerParams(
            collective_id=0, has_side_effects=True, vmem_limit_bytes=56 * 2**20
        ),
        name="clip_attention_backward",
    )(
        queries,
        keys,
        values,
        attention_out,
        output_grad,
        log_norm,
        layer_input,
        doc_start.reshape(1, T),
        visible_blocks,
    )


def solution(mesh):
    both = ("inner", "outer")
    return jax.shard_map(
        on_device,
        mesh=mesh,
        in_specs=(
            P(both, None),
            P(both, None),
            P(both, None),
            P(both, None),
            P(both, None),
            P(None, both),
            P(both, None),
            P(both),
            P(both, None),
        ),
        out_specs=(P(both, None), P(both, None)),
        check_vma=False,
    )
```

```python
import math

import jax
import jax.numpy as jnp
from jax import lax
from jax.experimental import pallas as pl
from jax.experimental.pallas import tpu as pltpu
from jax.sharding import PartitionSpec as P

D = 5120
HD = 128
HQ = 5
T = 128
Y, Z, X, C = 4, 8, 4, 2
N = Y * Z * X * C
GROUP = 4
UNIT = D // GROUP
HALF = UNIT // C
ROWS = D // N
PAIR = C * ROWS
EARLY = 32
FAR = 1.0e9
MESH = pl.DeviceIdType.MESH
f32, bf16 = jnp.float32, jnp.bfloat16
SCALE = 1.0 / math.sqrt(HD)
LOG2E = math.log2(math.e)


def place(y, z, x, c):
    return {"inner": y, "outer": (z * X + x) * C + c}


def dot(a, b, dims):
    return lax.dot_general(a, b, (dims, ((), ())), preferred_element_type=f32)


def kernel(
    q_hbm,
    k_hbm,
    v_hbm,
    o_hbm,
    do_hbm,
    lse_hbm,
    x_hbm,
    start_hbm,
    vis_hbm,
    w_ref,
    dq_ref,
    lse_ref,
    start_ref,
    vis_ref,
    q_all,
    do_all,
    o_own,
    kbuf,
    vbuf,
    stat,
    p_buf,
    p_half,
    ds_buf,
    ret_send,
    ret_recv,
    dq_part,
    dq_recv,
    x_recv,
    xt,
    own,
    g_all,
    acc,
    rs_send,
    rs_recv,
    wsum,
    sq1,
    sq2,
    load_sem,
    qx_s,
    qx_r,
    kv_s,
    kv_r,
    ret_s,
    ret_r,
    x_s,
    x_r,
    g_s,
    g_r,
    dq_s,
    dq_r,
    rs_s,
    rs_r,
    w_s,
    w_r,
    sq_s,
    sq_r,
    wave,
):
    y = lax.axis_index("inner")
    outer = lax.axis_index("outer")
    z = outer // (X * C)
    x = (outer // C) % X
    c = outer % C
    other = 1 - c
    block = y * (Z * X * C) + outer
    sib = place(y, z, x, other)
    taker = z // (Z // C) == c
    dz = jnp.where(c == 0, 1, Z - 1)
    chips = [(y, z), (lax.rem(y + 1, Y), z), (lax.rem(y + Y - 1, Y), z), (y, lax.rem(z + dz, Z))]
    peers = [(i, *chips[i], cc) for i in (1, 2, 3) for cc in range(C)]
    peers.append((0, y, z, other))
    named = [c * GROUP + i for i in range(GROUP)]
    arrivals = [other * GROUP, *[cs * GROUP + i for i in (1, 2, 3) for cs in range(C)]]

    def unit_owner(yy, zz):
        return lax.rem(yy + 2 * zz + 1, Y)

    def block_at(step):
        b = lax.rem(block + (step + N), N)
        return {"inner": b // (Z * X * C), "outer": lax.rem(b, Z * X * C)}

    def send(src, dst, ssem, rsem, device):
        copy = pltpu.make_async_remote_copy(
            src_ref=src, dst_ref=dst, send_sem=ssem, recv_sem=rsem, device_id=device, device_id_type=MESH
        )
        return copy

    barrier = pltpu.get_barrier_semaphore()

    def greet(device):
        pl.semaphore_signal(barrier, inc=1, device_id=device, device_id_type=MESH)

    z_steps = [[place(y, lax.rem(z + dz, Z), x, c) for dz in dzs] for dzs in ((1, Z - 1), (2, Z - 2))]
    x_steps = [place(y, z, lax.rem(x + dx, X), c) for dx in range(1, X)]
    y_steps = [place(lax.rem(y + dy, Y), z, x, c) for dy in (1, Y - 1)]
    waves = [z_steps[0], z_steps[1], x_steps, y_steps]
    near = [*[block_at(step) for step in (-4, 4, -2, 2)], *x_steps, *y_steps, *z_steps[0]]
    near += [place(yy, z, x, other) for yy in (lax.rem(y + 1, Y), lax.rem(y + Y - 1, Y))]
    near += [place(y, zz, x, other) for zz in (lax.rem(z + 1, Z), lax.rem(z + Z - 1, Z))]
    near.append(sib)
    for device in near:
        greet(device)

    def wave_out(k):
        for device in waves[k]:
            pl.semaphore_signal(wave.at[k], inc=1, device_id=device, device_id_type=MESH)

    def wave_in(k):
        pl.semaphore_wait(wave.at[k], len(waves[k]))

    late = []
    loads = [
        pltpu.make_async_copy(do_hbm, do_all.at[c], load_sem.at[0]),
        pltpu.make_async_copy(o_hbm, o_own, load_sem.at[1]),
        pltpu.make_async_copy(q_hbm, q_all.at[c], load_sem.at[2]),
        pltpu.make_async_copy(k_hbm, kbuf.at[0], load_sem.at[3]),
        pltpu.make_async_copy(v_hbm, vbuf.at[0], load_sem.at[4]),
        pltpu.make_async_copy(lse_hbm, lse_ref, load_sem.at[6]),
        pltpu.make_async_copy(start_hbm, start_ref, load_sem.at[7]),
        pltpu.make_async_copy(vis_hbm, vis_ref, load_sem.at[8]),
    ]
    for load in loads:
        load.start()

    pl.semaphore_wait(barrier, len(near))

    cp_q = send(q_hbm, q_all.at[c], qx_s.at[0], qx_r.at[0], sib)
    cp_do = send(do_hbm, do_all.at[c], qx_s.at[1], qx_r.at[1], sib)
    cp_st = send(stat.at[c], stat.at[c], qx_s.at[2], qx_r.at[2], sib)
    cp_k, cp_v = [
        [send(src, buf.at[j], kv_s.at[2 * n + j - 1], kv_r.at[2 * n + j - 1], block_at(2 * j)) for j in (1, 2)]
        for n, (src, buf) in enumerate(((k_hbm, kbuf), (v_hbm, vbuf)))
    ]
    for copy in [*cp_k, cp_q, cp_do, *cp_v]:
        copy.start()

    def x_cols(yy, zz, cc):
        return x_hbm.at[:, pl.ds(pl.multiple_of(unit_owner(yy, zz) * UNIT + cc * HALF, HD), HALF)]

    x_own = pltpu.make_async_copy(x_cols(y, z, c), x_recv.at[named[0]], load_sem.at[5])
    x_own.start()
    cp_x = []
    for i, yy, zz, cc in peers:
        at = named[i]
        copy = send(x_cols(yy, zz, cc), x_recv.at[at], x_s.at[i * C + cc], x_r.at[at], place(yy, zz, x, cc))
        copy.start()
        cp_x.append(copy)

    for i in (0, 1, 5, 6, 7):
        loads[i].wait()
    for h in range(HQ):
        cols = pl.ds(h * HD, HD)
        prod = do_all[c, :, cols].astype(f32) * o_own[:, cols].astype(f32)
        stat[c, pl.ds(h, 1), :] = jnp.sum(prod.T, axis=0, keepdims=True)
    stat[c, pl.ds(HQ, HQ), :] = lse_ref[...] * LOG2E
    first = start_ref[...].astype(f32)
    for d in range(5):
        kb = block - d
        wanted = jnp.where(kb >= 0, kb, -7)
        hit = jnp.max(jnp.where(vis_ref[...] == wanted, 1.0, 0.0), axis=1, keepdims=True)
        stat[c, pl.ds(10 + d, 1), :] = jnp.where(hit > 0.5, first, FAR)
    stat[c, pl.ds(15, 1), :] = jnp.full((1, T), FAR, f32)
    cp_st.start()
    wave_out(0)

    for load in loads[2:5]:
        load.wait()
    cp_q.wait_recv()
    cp_do.wait_recv()
    cp_st.wait_recv()

    def row(r):
        return jnp.concatenate([stat[0, pl.ds(r, 1), :], stat[1, pl.ds(r, 1), :]], axis=1)


    def lowest(j):
        lows = []
        for i in range(C):
            d0, d1 = i + 2 * j, i - 1 + 2 * j
            at0, at1 = 10 + min(d0, 5), 10 + (d1 if d1 >= 0 else 5)
            lows.append(jnp.where(c == 0, stat[i, pl.ds(at0, 1), :], stat[i, pl.ds(at1, 1), :]))
        return jnp.concatenate(lows, axis=1)

    def heads(ref, h):
        return ref[:, :, pl.ds(h * HD, HD)].reshape(2 * T, HD)

    def probs(first, count):
        rows = pl.ds(first * T, count * T)
        iota_u = lax.broadcasted_iota(jnp.int32, (count * T, 2 * T), 0)
        iota_t = lax.broadcasted_iota(jnp.int32, (count * T, 2 * T), 1)
        key_pos = (block - 2 * first) * T + iota_u
        low = lowest(first)
        if count == 2:
            key_pos = jnp.where(iota_u < T, key_pos, key_pos - 3 * T)
            low = jnp.where(iota_u < T, low, lowest(first + 1))
        allowed = (key_pos.astype(f32) >= low) & (key_pos <= (block - c) * T + iota_t)
        key_rows = kbuf[first : first + count].reshape(count * T, HD)
        for h in range(HQ):
            s = dot(key_rows, heads(q_all, h), ((1,), (1,)))
            prob = jnp.where(allowed, jnp.exp2(s * (SCALE * LOG2E) - row(HQ + h)), 0.0)
            p_buf[h, rows, :] = prob
            p_half[h, rows, :] = prob.astype(bf16)
        part = jnp.zeros((count * T, HD), f32)
        for h in range(HQ):
            part += dot(p_half[h, rows, :], heads(do_all, h), ((1,), (0,)))
        return part

    def score_grads(first, count):
        rows = pl.ds(first * T, count * T)
        value_rows = vbuf[first : first + count].reshape(count * T, HD)
        for h in range(HQ):
            dp = dot(value_rows, heads(do_all, h), ((1,), (1,)))
            ds_buf[h, rows, :] = (p_buf[h, rows, :] * (dp - row(h)) * SCALE).astype(bf16)
        part = jnp.zeros((count * T, HD), f32)
        for h in range(HQ):
            part += dot(ds_buf[h, rows, :], heads(q_all, h), ((1,), (0,)))
        return part

    def give_back(n, part):
        for j in (2, 1):
            k = 2 * n + j - 1
            ret_send[k] = part[(j - 1) * T : j * T].astype(bf16)
            copy = send(ret_send.at[k], ret_recv.at[k], ret_s.at[k], ret_r.at[k], block_at(-2 * j))
            copy.start()
            cp_ret.append(copy)

    cp_ret = []
    own[0] = probs(0, 1)
    own[1] = score_grads(0, 1)
    wave_in(0)
    wave_out(1)
    for copy in cp_k:
        copy.wait_recv()
    give_back(0, probs(1, 2))
    for copy in cp_v:
        copy.wait_recv()
    give_back(1, score_grads(1, 2))

    wave_in(1)
    wave_out(2)
    key_cat = kbuf[...].reshape(3 * T, HD)
    for h in range(HQ):
        part = dot(ds_buf[h], key_cat, ((0,), (0,)))
        dq_part[0, :, pl.ds(h * HD, HD)] = part[:T]
        dq_part[1, :, pl.ds(h * HD, HD)] = part[T:]
    cp_dq = send(dq_part.at[other], dq_recv, dq_s.at[0], dq_r.at[0], sib)
    cp_dq.start()

    cp_g = []
    for n in range(2):
        cp_ret[2 * n].wait_recv()
        cp_ret[2 * n + 1].wait_recv()
        mine = g_all.at[n, named[0]]
        g_all[n, named[0]] = (own[n] + ret_recv[2 * n].astype(f32) + ret_recv[2 * n + 1].astype(f32)).astype(bf16)
        for i, yy, zz, cc in peers:
            at = named[i]
            copy = send(mine, g_all.at[n, at], g_s.at[n, i * C + cc], g_r.at[n, at], place(yy, zz, x, cc))
            copy.start()
            cp_g.append(copy)
        if n == 0:
            wave_in(2)
            wave_out(3)
            cp_dq.wait_recv()
            dq_ref[...] = (dq_part[c] + dq_recv[...]).astype(bf16)

    x_own.wait()
    for at in arrivals:
        send(x_recv.at[at], x_recv.at[at], x_s.at[0], x_r.at[at], sib).wait_recv()
    for m in range(C * GROUP):
        xt[m // 2, :, pl.ds(m % 2 * T, T)] = x_recv[m].T

    slot = z * X + x
    to_y = unit_owner(y, z)
    shares = (pl.ds(0, EARLY), pl.ds(EARLY, 2 * PAIR - EARLY))
    step = PAIR * X
    for n in range(2):
        for at in arrivals:
            send(g_all.at[n, at], g_all.at[n, at], g_s.at[n, 0], g_r.at[n, at], sib).wait_recv()
        if n == 0:
            wave_in(3)
        for i in range(Z // C):
            kz = lax.rem(z + 2 + i, Z // C)
            rows = pl.ds(pl.multiple_of(kz * step, step), step)
            total = dot(xt[0, rows, :], g_all[n, 0:2].reshape(2 * T, HD), ((1,), (0,)))
            for m in range(2, C * GROUP, 2):
                total += dot(xt[m // 2, rows, :], g_all[n, m : m + 2].reshape(2 * T, HD), ((1,), (0,)))
            acc[n, rows, :] = total
            for k in range(X):
                kx = lax.rem(x + 2 + k, X)
                m = kz * X + kx
                at = pl.multiple_of(m * PAIR, PAIR)
                if n == 0:
                    part = acc[0, pl.ds(at, EARLY), :]
                else:
                    left = acc[0, pl.ds(pl.multiple_of(at + EARLY, 8), PAIR - EARLY), :]
                    part = jnp.concatenate([left, acc[1, pl.ds(at, PAIR), :]], axis=0)
                rs_send[m, shares[n], :] = part.astype(bf16)
                to = place(to_y, c * (Z // C) + kz, kx, c)
                send(rs_send.at[m, shares[n]], rs_recv.at[slot, shares[n]], rs_s.at[n], rs_r.at[n], to).start()

    def rs_left():
        for n, rows in enumerate(shares):
            some = rs_recv.at[pl.ds(0, Z // C * X), rows]
            send(rs_send.at[:, rows], some, rs_s.at[n], rs_r.at[n], sib).wait_send()

    late.append(rs_left)
    cp_w = send(wsum, wsum, w_s.at[0], w_r.at[0], sib)
    some_xy = pl.ds(1, Y * X - 1)
    all_xy = send(sq1.at[some_xy], sq1.at[some_xy], sq_s.at[0], sq_r.at[0], sib)
    some_zc = send(sq2.at[pl.ds(0, Z - 1)], sq2.at[pl.ds(0, Z - 1)], sq_s.at[1], sq_r.at[1], sib)
    all_zc = send(sq2, sq2, sq_s.at[1], sq_r.at[1], sib)

    def send_xy(i, _):
        to = place(lax.rem(y + i // X, Y), z, lax.rem(x + lax.rem(i, X), X), c)
        send(sq1.at[0], sq1.at[i], sq_s.at[0], sq_r.at[0], to).start()
        return 0

    def send_zc(i, _):
        to = place(y, lax.rem(z + Z // 2 + i // C, Z), x, lax.rem(c + 1 + lax.rem(i, C), C))

        @pl.when(i != Z + 1)
        def _():
            send(sq2.at[z], sq2.at[z], sq_s.at[1], sq_r.at[1], to).start()

        return 0

    @pl.when(taker)
    def _():
        squares = jnp.zeros((1, HD), f32)
        for n, rows in enumerate(shares):
            here = rs_recv.at[:, rows]
            send(here, here, rs_s.at[n], rs_r.at[n], sib).wait_recv()
            total = rs_recv[0, rows, :].astype(f32)
            for i in range(1, Z * X):
                total += rs_recv[i, rows, :].astype(f32)
            wsum[rows, :] = total
            squares += jnp.sum(total * total, axis=0, keepdims=True)
        cp_w.start()
        sq1[0] = squares
        lax.fori_loop(1, Y * X, send_xy, 0)
        all_xy.wait_recv()
        sq2[z] = jnp.sum(sq1[...], axis=0)
        lax.fori_loop(0, Z * C, send_zc, 0)
        some_zc.wait_recv()

    @pl.when(jnp.logical_not(taker))
    def _():
        cp_w.wait_recv()
        all_zc.wait_recv()

    def sums_left():
        @pl.when(taker)
        def _():
            cp_w.wait_send()
            all_xy.wait_send()
            for part in (pl.ds(0, Z), pl.ds(0, Z - 1)):
                send(sq2.at[part], sq2.at[part], sq_s.at[1], sq_r.at[1], sib).wait_send()

    late.append(sums_left)
    halves = []
    for k in range(C):
        at, then = pl.ds(k * ROWS, ROWS), pl.ds(PAIR + k * ROWS, ROWS)
        halves.append(jnp.concatenate([wsum[then, :], wsum[at, :]], axis=1))
    rows_sum = jnp.where(c == 0, halves[0], halves[1])

    lanes = jnp.sum(sq2[...], axis=0)
    square_total = jnp.sum(lanes, axis=1, keepdims=True)
    limit = math.sqrt(D * 2 * HD)
    clip = jnp.minimum(1.0, limit / (jnp.sqrt(square_total) + 1e-6))
    w_ref[...] = rows_sum * clip

    for copy in [cp_q, cp_do, cp_st, *cp_k, *cp_v, *cp_x, *cp_ret, cp_dq, *cp_g]:
        copy.wait_send()

    for wait in late:
        wait()


def on_device(queries, keys, values, attention_out, output_grad, log_norm, layer_input, doc_start, visible_blocks):
    hbm = pl.BlockSpec(memory_space=pl.ANY)
    dma = pltpu.SemaphoreType.DMA
    return pl.pallas_call(
        kernel,
        out_shape=(pltpu.VMEM((ROWS, 2 * HD), f32), pltpu.VMEM((T, HQ * HD), bf16)),
        in_specs=[hbm] * 9,
        out_specs=(pl.BlockSpec(memory_space=pltpu.VMEM),) * 2,
        scratch_shapes=[
            pltpu.VMEM((HQ, T), f32),
            pltpu.VMEM((1, T), jnp.int32),
            pltpu.VMEM((1, 5), jnp.int32),
            pltpu.VMEM((C, T, HQ * HD), bf16),
            pltpu.VMEM((C, T, HQ * HD), bf16),
            pltpu.VMEM((T, HQ * HD), bf16),
            pltpu.VMEM((3, T, HD), bf16),
            pltpu.VMEM((3, T, HD), bf16),
            pltpu.VMEM((C, 16, T), f32),
            pltpu.VMEM((HQ, 3 * T, 2 * T), f32),
            pltpu.VMEM((HQ, 3 * T, 2 * T), bf16),
            pltpu.VMEM((HQ, 3 * T, 2 * T), bf16),
            pltpu.VMEM((4, T, HD), bf16),
            pltpu.VMEM((4, T, HD), bf16),
            pltpu.VMEM((C, T, HQ * HD), f32),
            pltpu.VMEM((T, HQ * HD), f32),
            pltpu.VMEM((C * GROUP, T, HALF), bf16),
            pltpu.VMEM((GROUP, HALF, C * T), bf16),
            pltpu.VMEM((2, T, HD), f32),
            pltpu.VMEM((2, C * GROUP, T, HD), bf16),
            pltpu.VMEM((2, HALF, HD), f32),
            pltpu.VMEM((Z // C * X, 2 * PAIR, HD), bf16),
            pltpu.VMEM((Z * X, 2 * PAIR, HD), bf16),
            pltpu.VMEM((2 * PAIR, HD), f32),
            pltpu.VMEM((Y * X, 1, HD), f32),
            pltpu.VMEM((Z, 1, HD), f32),
            dma((9,)),
            dma((3,)),
            dma((3,)),
            dma((4,)),
            dma((4,)),
            dma((4,)),
            dma((4,)),
            dma((C * GROUP,)),
            dma((C * GROUP,)),
            dma((2, C * GROUP)),
            dma((2, C * GROUP)),
            dma((1,)),
            dma((1,)),
            dma((2,)),
            dma((2,)),
            dma((1,)),
            dma((1,)),
            dma((2,)),
            dma((2,)),
            pltpu.SemaphoreType.REGULAR((4,)),
        ],
        compiler_params=pltpu.CompilerParams(
            collective_id=0, has_side_effects=True, vmem_limit_bytes=56 * 2**20
        ),
        name="clip_attention_backward",
    )(
        queries,
        keys,
        values,
        attention_out,
        output_grad,
        log_norm,
        layer_input,
        doc_start.reshape(1, T),
        visible_blocks,
    )


def solution(mesh):
    both = ("inner", "outer")
    return jax.shard_map(
        on_device,
        mesh=mesh,
        in_specs=(
            P(both, None),
            P(both, None),
            P(both, None),
            P(both, None),
            P(both, None),
            P(None, both),
            P(both, None),
            P(both),
            P(both, None),
        ),
        out_specs=(P(both, None), P(both, None)),
        check_vma=False,
    )
```

```python
import math

import jax
import jax.numpy as jnp
from jax import lax
from jax.experimental import pallas as pl
from jax.experimental.pallas import tpu as pltpu
from jax.sharding import PartitionSpec as P

D = 5120
HD = 128
HQ = 5
T = 128
Y, Z, X, C = 4, 8, 4, 2
N = Y * Z * X * C
GROUP = 4
UNIT = D // GROUP
HALF = UNIT // C
ROWS = D // N
PAIR = C * ROWS
EARLY = 32
FAR = 1.0e9
MESH = pl.DeviceIdType.MESH
f32, bf16 = jnp.float32, jnp.bfloat16
SCALE = 1.0 / math.sqrt(HD)
LOG2E = math.log2(math.e)


def place(y, z, x, c):
    return {"inner": y, "outer": (z * X + x) * C + c}


def dot(a, b, dims):
    return lax.dot_general(a, b, (dims, ((), ())), preferred_element_type=f32)


def kernel(
    q_hbm,
    k_hbm,
    v_hbm,
    o_hbm,
    do_hbm,
    lse_hbm,
    x_hbm,
    start_hbm,
    vis_hbm,
    w_ref,
    dq_ref,
    lse_ref,
    start_ref,
    vis_ref,
    q_all,
    do_all,
    o_own,
    kbuf,
    vbuf,
    stat,
    p_buf,
    p_half,
    ds_buf,
    ret_send,
    ret_recv,
    dq_part,
    dq_recv,
    x_recv,
    xt,
    own,
    g_all,
    acc,
    rs_send,
    rs_recv,
    wsum,
    sq1,
    sq2,
    load_sem,
    qx_s,
    qx_r,
    kv_s,
    kv_r,
    ret_s,
    ret_r,
    x_s,
    x_r,
    g_s,
    g_r,
    dq_s,
    dq_r,
    rs_s,
    rs_r,
    w_s,
    w_r,
    sq_s,
    sq_r,
    wave,
):
    y = lax.axis_index("inner")
    outer = lax.axis_index("outer")
    z = outer // (X * C)
    x = (outer // C) % X
    c = outer % C
    other = 1 - c
    block = y * (Z * X * C) + outer
    sib = place(y, z, x, other)
    taker = z // (Z // C) == c
    dz = jnp.where(c == 0, 1, Z - 1)
    chips = [(y, z), (lax.rem(y + 1, Y), z), (lax.rem(y + Y - 1, Y), z), (y, lax.rem(z + dz, Z))]
    peers = [(i, *chips[i], cc) for i in (1, 2, 3) for cc in range(C)]
    peers.append((0, y, z, other))
    named = [c * GROUP + i for i in range(GROUP)]
    arrivals = [other * GROUP, *[cs * GROUP + i for i in (1, 2, 3) for cs in range(C)]]

    def unit_owner(yy, zz):
        return lax.rem(yy + 2 * zz + 1, Y)

    def block_at(step):
        b = lax.rem(block + (step + N), N)
        return {"inner": b // (Z * X * C), "outer": lax.rem(b, Z * X * C)}

    def send(src, dst, ssem, rsem, device):
        copy = pltpu.make_async_remote_copy(
            src_ref=src, dst_ref=dst, send_sem=ssem, recv_sem=rsem, device_id=device, device_id_type=MESH
        )
        return copy

    barrier = pltpu.get_barrier_semaphore()

    def greet(device):
        pl.semaphore_signal(barrier, inc=1, device_id=device, device_id_type=MESH)

    z_steps = [[place(y, lax.rem(z + dz, Z), x, c) for dz in dzs] for dzs in ((1, Z - 1), (2, Z - 2))]
    x_steps = [place(y, z, lax.rem(x + dx, X), c) for dx in range(1, X)]
    y_steps = [place(lax.rem(y + dy, Y), z, x, c) for dy in (1, Y - 1)]
    waves = [z_steps[0], z_steps[1], x_steps, y_steps]
    near = [*[block_at(step) for step in (-4, 4, -2, 2)], *x_steps, *y_steps, *z_steps[0]]
    near += [place(yy, z, x, other) for yy in (lax.rem(y + 1, Y), lax.rem(y + Y - 1, Y))]
    near += [place(y, zz, x, other) for zz in (lax.rem(z + 1, Z), lax.rem(z + Z - 1, Z))]
    near.append(sib)
    for device in near:
        greet(device)

    def wave_out(k):
        for device in waves[k]:
            pl.semaphore_signal(wave.at[k], inc=1, device_id=device, device_id_type=MESH)

    def wave_in(k):
        pl.semaphore_wait(wave.at[k], len(waves[k]))

    late = []
    loads = [
        pltpu.make_async_copy(do_hbm, do_all.at[c], load_sem.at[0]),
        pltpu.make_async_copy(o_hbm, o_own, load_sem.at[1]),
        pltpu.make_async_copy(q_hbm, q_all.at[c], load_sem.at[2]),
        pltpu.make_async_copy(k_hbm, kbuf.at[0], load_sem.at[3]),
        pltpu.make_async_copy(v_hbm, vbuf.at[0], load_sem.at[4]),
        pltpu.make_async_copy(lse_hbm, lse_ref, load_sem.at[6]),
        pltpu.make_async_copy(start_hbm, start_ref, load_sem.at[7]),
        pltpu.make_async_copy(vis_hbm, vis_ref, load_sem.at[8]),
    ]
    for load in loads:
        load.start()

    pl.semaphore_wait(barrier, len(near))

    cp_q = send(q_hbm, q_all.at[c], qx_s.at[0], qx_r.at[0], sib)
    cp_do = send(do_hbm, do_all.at[c], qx_s.at[1], qx_r.at[1], sib)
    cp_st = send(stat.at[c], stat.at[c], qx_s.at[2], qx_r.at[2], sib)
    cp_k, cp_v = [
        [send(src, buf.at[j], kv_s.at[2 * n + j - 1], kv_r.at[2 * n + j - 1], block_at(2 * j)) for j in (1, 2)]
        for n, (src, buf) in enumerate(((k_hbm, kbuf), (v_hbm, vbuf)))
    ]
    for copy in [*cp_k, cp_q, cp_do, *cp_v]:
        copy.start()

    def x_cols(yy, zz, cc):
        return x_hbm.at[:, pl.ds(pl.multiple_of(unit_owner(yy, zz) * UNIT + cc * HALF, HD), HALF)]

    x_own = pltpu.make_async_copy(x_cols(y, z, c), x_recv.at[named[0]], load_sem.at[5])
    x_own.start()
    cp_x = []
    for i, yy, zz, cc in peers:
        at = named[i]
        copy = send(x_cols(yy, zz, cc), x_recv.at[at], x_s.at[i * C + cc], x_r.at[at], place(yy, zz, x, cc))
        copy.start()
        cp_x.append(copy)

    for i in (0, 1, 5, 6, 7):
        loads[i].wait()
    for h in range(HQ):
        cols = pl.ds(h * HD, HD)
        prod = do_all[c, :, cols].astype(f32) * o_own[:, cols].astype(f32)
        stat[c, pl.ds(h, 1), :] = jnp.sum(prod.T, axis=0, keepdims=True)
    stat[c, pl.ds(HQ, HQ), :] = lse_ref[...] * LOG2E
    first = start_ref[...].astype(f32)
    for d in range(5):
        kb = block - d
        wanted = jnp.where(kb >= 0, kb, -7)
        hit = jnp.max(jnp.where(vis_ref[...] == wanted, 1.0, 0.0), axis=1, keepdims=True)
        stat[c, pl.ds(10 + d, 1), :] = jnp.where(hit > 0.5, first, FAR)
    stat[c, pl.ds(15, 1), :] = jnp.full((1, T), FAR, f32)
    cp_st.start()
    wave_out(0)

    for load in loads[2:5]:
        load.wait()
    cp_q.wait_recv()
    cp_do.wait_recv()
    cp_st.wait_recv()

    def row(r):
        return jnp.concatenate([stat[0, pl.ds(r, 1), :], stat[1, pl.ds(r, 1), :]], axis=1)


    def lowest(j):
        lows = []
        for i in range(C):
            d0, d1 = i + 2 * j, i - 1 + 2 * j
            at0, at1 = 10 + min(d0, 5), 10 + (d1 if d1 >= 0 else 5)
            lows.append(jnp.where(c == 0, stat[i, pl.ds(at0, 1), :], stat[i, pl.ds(at1, 1), :]))
        return jnp.concatenate(lows, axis=1)

    def heads(ref, h):
        return ref[:, :, pl.ds(h * HD, HD)].reshape(2 * T, HD)

    def probs(first, count):
        rows = pl.ds(first * T, count * T)
        iota_u = lax.broadcasted_iota(jnp.int32, (count * T, 2 * T), 0)
        iota_t = lax.broadcasted_iota(jnp.int32, (count * T, 2 * T), 1)
        key_pos = (block - 2 * first) * T + iota_u
        low = lowest(first)
        if count == 2:
            key_pos = jnp.where(iota_u < T, key_pos, key_pos - 3 * T)
            low = jnp.where(iota_u < T, low, lowest(first + 1))
        allowed = (key_pos.astype(f32) >= low) & (key_pos <= (block - c) * T + iota_t)
        key_rows = kbuf[first : first + count].reshape(count * T, HD)
        for h in range(HQ):
            s = dot(key_rows, heads(q_all, h), ((1,), (1,)))
            prob = jnp.where(allowed, jnp.exp2(s * (SCALE * LOG2E) - row(HQ + h)), 0.0)
            p_buf[h, rows, :] = prob
            p_half[h, rows, :] = prob.astype(bf16)
        part = jnp.zeros((count * T, HD), f32)
        for h in range(HQ):
            part += dot(p_half[h, rows, :], heads(do_all, h), ((1,), (0,)))
        return part

    def score_grads(first, count):
        rows = pl.ds(first * T, count * T)
        value_rows = vbuf[first : first + count].reshape(count * T, HD)
        for h in range(HQ):
            dp = dot(value_rows, heads(do_all, h), ((1,), (1,)))
            ds_buf[h, rows, :] = (p_buf[h, rows, :] * (dp - row(h)) * SCALE).astype(bf16)
        part = jnp.zeros((count * T, HD), f32)
        for h in range(HQ):
            part += dot(ds_buf[h, rows, :], heads(q_all, h), ((1,), (0,)))
        return part

    def give_back(n, part):
        for j in (2, 1):
            k = 2 * n + j - 1
            ret_send[k] = part[(j - 1) * T : j * T].astype(bf16)
            copy = send(ret_send.at[k], ret_recv.at[k], ret_s.at[k], ret_r.at[k], block_at(-2 * j))
            copy.start()
            cp_ret.append(copy)

    cp_ret = []
    own[0] = probs(0, 1)
    own[1] = score_grads(0, 1)
    wave_in(0)
    wave_out(1)
    for copy in cp_k:
        copy.wait_recv()
    give_back(0, probs(1, 2))
    for copy in cp_v:
        copy.wait_recv()
    give_back(1, score_grads(1, 2))

    wave_in(1)
    wave_out(2)
    key_cat = kbuf[...].reshape(3 * T, HD)
    for h in range(HQ):
        part = dot(ds_buf[h], key_cat, ((0,), (0,)))
        dq_part[0, :, pl.ds(h * HD, HD)] = part[:T]
        dq_part[1, :, pl.ds(h * HD, HD)] = part[T:]
    cp_dq = send(dq_part.at[other], dq_recv, dq_s.at[0], dq_r.at[0], sib)
    cp_dq.start()

    cp_g = []
    for n in range(2):
        cp_ret[2 * n].wait_recv()
        cp_ret[2 * n + 1].wait_recv()
        mine = g_all.at[n, named[0]]
        g_all[n, named[0]] = (own[n] + ret_recv[2 * n].astype(f32) + ret_recv[2 * n + 1].astype(f32)).astype(bf16)
        for i, yy, zz, cc in peers:
            at = named[i]
            copy = send(mine, g_all.at[n, at], g_s.at[n, i * C + cc], g_r.at[n, at], place(yy, zz, x, cc))
            copy.start()
            cp_g.append(copy)
        if n == 0:
            wave_in(2)
            wave_out(3)
            cp_dq.wait_recv()
            dq_ref[...] = (dq_part[c] + dq_recv[...]).astype(bf16)

    x_own.wait()
    for at in arrivals:
        send(x_recv.at[at], x_recv.at[at], x_s.at[0], x_r.at[at], sib).wait_recv()
    for m in range(C * GROUP):
        xt[m // 2, :, pl.ds(m % 2 * T, T)] = x_recv[m].T

    slot = z * X + x
    to_y = unit_owner(y, z)
    shares = (pl.ds(0, EARLY), pl.ds(EARLY, 2 * PAIR - EARLY))
    step = PAIR * X
    for n in range(2):
        for at in arrivals:
            send(g_all.at[n, at], g_all.at[n, at], g_s.at[n, 0], g_r.at[n, at], sib).wait_recv()
        if n == 0:
            wave_in(3)
        for i in range(Z // C):
            kz = lax.rem(z + 2 + i, Z // C)
            rows = pl.ds(pl.multiple_of(kz * step, step), step)
            total = dot(xt[0, rows, :], g_all[n, 0:2].reshape(2 * T, HD), ((1,), (0,)))
            for m in range(2, C * GROUP, 2):
                total += dot(xt[m // 2, rows, :], g_all[n, m : m + 2].reshape(2 * T, HD), ((1,), (0,)))
            acc[n, rows, :] = total
            for k in range(X):
                kx = lax.rem(x + 2 + k, X)
                m = kz * X + kx
                at = pl.multiple_of(m * PAIR, PAIR)
                if n == 0:
                    part = acc[0, pl.ds(at, EARLY), :]
                else:
                    left = acc[0, pl.ds(pl.multiple_of(at + EARLY, 8), PAIR - EARLY), :]
                    part = jnp.concatenate([left, acc[1, pl.ds(at, PAIR), :]], axis=0)
                rs_send[m, shares[n], :] = part.astype(bf16)
                to = place(to_y, c * (Z // C) + kz, kx, c)
                send(rs_send.at[m, shares[n]], rs_recv.at[slot, shares[n]], rs_s.at[n], rs_r.at[n], to).start()

    def rs_left():
        for n, rows in enumerate(shares):
            some = rs_recv.at[pl.ds(0, Z // C * X), rows]
            send(rs_send.at[:, rows], some, rs_s.at[n], rs_r.at[n], sib).wait_send()

    late.append(rs_left)
    cp_w = send(wsum, wsum, w_s.at[0], w_r.at[0], sib)
    some_xy = pl.ds(1, Y * X - 1)
    all_xy = send(sq1.at[some_xy], sq1.at[some_xy], sq_s.at[0], sq_r.at[0], sib)
    some_zc = send(sq2.at[pl.ds(0, Z - 1)], sq2.at[pl.ds(0, Z - 1)], sq_s.at[1], sq_r.at[1], sib)
    all_zc = send(sq2, sq2, sq_s.at[1], sq_r.at[1], sib)

    def far_first(places):
        return sorted(places, key=lambda steps: -sum(min(k, size - k) for k, size in zip(steps, (Y, Z, X, C))))

    def send_xy():
        for i, (dy, _, dx, _) in enumerate(far_first([(dy, 0, dx, 0) for dy in range(Y) for dx in range(X)])[:-1]):
            to = place(lax.rem(y + dy, Y), z, lax.rem(x + dx, X), c)
            send(sq1.at[0], sq1.at[1 + i], sq_s.at[0], sq_r.at[0], to).start()

    def send_zc():
        for _, dz, _, dc in far_first([(0, dz, 0, dc) for dz in range(Z) for dc in range(C)])[:-1]:
            to = place(y, lax.rem(z + dz, Z), x, lax.rem(c + dc, C))
            send(sq2.at[z], sq2.at[z], sq_s.at[1], sq_r.at[1], to).start()

    @pl.when(taker)
    def _():
        squares = jnp.zeros((1, HD), f32)
        for n, rows in enumerate(shares):
            here = rs_recv.at[:, rows]
            send(here, here, rs_s.at[n], rs_r.at[n], sib).wait_recv()
            total = rs_recv[0, rows, :].astype(f32)
            for i in range(1, Z * X):
                total += rs_recv[i, rows, :].astype(f32)
            wsum[rows, :] = total
            squares += jnp.sum(total * total, axis=0, keepdims=True)
        cp_w.start()
        sq1[0] = squares
        send_xy()
        all_xy.wait_recv()
        sq2[z] = jnp.sum(sq1[...], axis=0)
        send_zc()

    @pl.when(jnp.logical_not(taker))
    def _():
        cp_w.wait_recv()

    def sums_left():
        @pl.when(taker)
        def _():
            cp_w.wait_send()
            all_xy.wait_send()
            for part in (pl.ds(0, Z), pl.ds(0, Z - 1)):
                send(sq2.at[part], sq2.at[part], sq_s.at[1], sq_r.at[1], sib).wait_send()

    late.append(sums_left)
    halves = []
    for k in range(C):
        at, then = pl.ds(k * ROWS, ROWS), pl.ds(PAIR + k * ROWS, ROWS)
        halves.append(jnp.concatenate([wsum[then, :], wsum[at, :]], axis=1))
    w_ref[...] = jnp.where(c == 0, halves[0], halves[1])
    pl.when(taker)(some_zc.wait_recv)
    pl.when(jnp.logical_not(taker))(all_zc.wait_recv)

    lanes = jnp.sum(sq2[...], axis=0)
    square_total = jnp.sum(lanes, axis=1, keepdims=True)
    limit = math.sqrt(D * 2 * HD)
    clip = jnp.minimum(1.0, limit / (jnp.sqrt(square_total) + 1e-6))
    w_ref[...] *= clip

    for copy in [cp_q, cp_do, cp_st, *cp_k, *cp_v, *cp_x, *cp_ret, cp_dq, *cp_g]:
        copy.wait_send()

    for wait in late:
        wait()


def on_device(queries, keys, values, attention_out, output_grad, log_norm, layer_input, doc_start, visible_blocks):
    hbm = pl.BlockSpec(memory_space=pl.ANY)
    dma = pltpu.SemaphoreType.DMA
    return pl.pallas_call(
        kernel,
        out_shape=(pltpu.VMEM((ROWS, 2 * HD), f32), pltpu.VMEM((T, HQ * HD), bf16)),
        in_specs=[hbm] * 9,
        out_specs=(pl.BlockSpec(memory_space=pltpu.VMEM),) * 2,
        scratch_shapes=[
            pltpu.VMEM((HQ, T), f32),
            pltpu.VMEM((1, T), jnp.int32),
            pltpu.VMEM((1, 5), jnp.int32),
            pltpu.VMEM((C, T, HQ * HD), bf16),
            pltpu.VMEM((C, T, HQ * HD), bf16),
            pltpu.VMEM((T, HQ * HD), bf16),
            pltpu.VMEM((3, T, HD), bf16),
            pltpu.VMEM((3, T, HD), bf16),
            pltpu.VMEM((C, 16, T), f32),
            pltpu.VMEM((HQ, 3 * T, 2 * T), f32),
            pltpu.VMEM((HQ, 3 * T, 2 * T), bf16),
            pltpu.VMEM((HQ, 3 * T, 2 * T), bf16),
            pltpu.VMEM((4, T, HD), bf16),
            pltpu.VMEM((4, T, HD), bf16),
            pltpu.VMEM((C, T, HQ * HD), f32),
            pltpu.VMEM((T, HQ * HD), f32),
            pltpu.VMEM((C * GROUP, T, HALF), bf16),
            pltpu.VMEM((GROUP, HALF, C * T), bf16),
            pltpu.VMEM((2, T, HD), f32),
            pltpu.VMEM((2, C * GROUP, T, HD), bf16),
            pltpu.VMEM((2, HALF, HD), f32),
            pltpu.VMEM((Z // C * X, 2 * PAIR, HD), bf16),
            pltpu.VMEM((Z * X, 2 * PAIR, HD), bf16),
            pltpu.VMEM((2 * PAIR, HD), f32),
            pltpu.VMEM((Y * X, 1, HD), f32),
            pltpu.VMEM((Z, 1, HD), f32),
            dma((9,)),
            dma((3,)),
            dma((3,)),
            dma((4,)),
            dma((4,)),
            dma((4,)),
            dma((4,)),
            dma((C * GROUP,)),
            dma((C * GROUP,)),
            dma((2, C * GROUP)),
            dma((2, C * GROUP)),
            dma((1,)),
            dma((1,)),
            dma((2,)),
            dma((2,)),
            dma((1,)),
            dma((1,)),
            dma((2,)),
            dma((2,)),
            pltpu.SemaphoreType.REGULAR((4,)),
        ],
        compiler_params=pltpu.CompilerParams(
            collective_id=0, has_side_effects=True, vmem_limit_bytes=56 * 2**20
        ),
        name="clip_attention_backward",
    )(
        queries,
        keys,
        values,
        attention_out,
        output_grad,
        log_norm,
        layer_input,
        doc_start.reshape(1, T),
        visible_blocks,
    )


def solution(mesh):
    both = ("inner", "outer")
    return jax.shard_map(
        on_device,
        mesh=mesh,
        in_specs=(
            P(both, None),
            P(both, None),
            P(both, None),
            P(both, None),
            P(both, None),
            P(None, both),
            P(both, None),
            P(both),
            P(both, None),
        ),
        out_specs=(P(both, None), P(both, None)),
        check_vma=False,
    )
```

```python
import math

import jax
import jax.numpy as jnp
from jax import lax
from jax.experimental import pallas as pl
from jax.experimental.pallas import tpu as pltpu
from jax.sharding import PartitionSpec as P

D = 5120
HD = 128
HQ = 5
T = 128
Y, Z, X, C = 4, 8, 4, 2
N = Y * Z * X * C
GROUP = 4
UNIT = D // GROUP
HALF = UNIT // C
ROWS = D // N
PAIR = C * ROWS
EARLY = 32
FAR = 1.0e9
MESH = pl.DeviceIdType.MESH
f32, bf16 = jnp.float32, jnp.bfloat16
SCALE = 1.0 / math.sqrt(HD)
LOG2E = math.log2(math.e)


def place(y, z, x, c):
    return {"inner": y, "outer": (z * X + x) * C + c}


def dot(a, b, dims):
    return lax.dot_general(a, b, (dims, ((), ())), preferred_element_type=f32)


def kernel(
    q_hbm,
    k_hbm,
    v_hbm,
    o_hbm,
    do_hbm,
    lse_hbm,
    x_hbm,
    start_hbm,
    vis_hbm,
    w_ref,
    dq_ref,
    lse_ref,
    start_ref,
    vis_ref,
    q_all,
    do_all,
    o_own,
    kbuf,
    vbuf,
    stat,
    p_buf,
    p_half,
    ds_buf,
    ret_send,
    ret_recv,
    dq_part,
    dq_recv,
    x_recv,
    xt,
    own,
    g_all,
    acc,
    rs_send,
    rs_recv,
    wsum,
    sq1,
    sq2,
    load_sem,
    qx_s,
    qx_r,
    kv_s,
    kv_r,
    ret_s,
    ret_r,
    x_s,
    x_r,
    g_s,
    g_r,
    dq_s,
    dq_r,
    rs_s,
    rs_r,
    w_s,
    w_r,
    sq_s,
    sq_r,
    wave,
):
    y = lax.axis_index("inner")
    outer = lax.axis_index("outer")
    z = outer // (X * C)
    x = (outer // C) % X
    c = outer % C
    other = 1 - c
    block = y * (Z * X * C) + outer
    sib = place(y, z, x, other)
    taker = z // (Z // C) == c
    dz = jnp.where(c == 0, 1, Z - 1)
    chips = [(y, z), (lax.rem(y + 1, Y), z), (lax.rem(y + Y - 1, Y), z), (y, lax.rem(z + dz, Z))]
    peers = [(i, *chips[i], cc) for i in (1, 2, 3) for cc in range(C)]
    peers.append((0, y, z, other))
    named = [c * GROUP + i for i in range(GROUP)]
    arrivals = [other * GROUP, *[cs * GROUP + i for i in (1, 2, 3) for cs in range(C)]]

    def unit_owner(yy, zz):
        return lax.rem(yy + 2 * zz + 1, Y)

    def block_at(step):
        b = lax.rem(block + (step + N), N)
        return {"inner": b // (Z * X * C), "outer": lax.rem(b, Z * X * C)}

    def send(src, dst, ssem, rsem, device):
        copy = pltpu.make_async_remote_copy(
            src_ref=src, dst_ref=dst, send_sem=ssem, recv_sem=rsem, device_id=device, device_id_type=MESH
        )
        return copy

    barrier = pltpu.get_barrier_semaphore()

    def greet(device):
        pl.semaphore_signal(barrier, inc=1, device_id=device, device_id_type=MESH)

    z_steps = [[place(y, lax.rem(z + dz, Z), x, c) for dz in dzs] for dzs in ((1, Z - 1), (2, Z - 2))]
    x_steps = [place(y, z, lax.rem(x + dx, X), c) for dx in range(1, X)]
    y_steps = [place(lax.rem(y + dy, Y), z, x, c) for dy in (1, Y - 1)]
    waves = [z_steps[0], z_steps[1], x_steps, y_steps]
    near = [*[block_at(step) for step in (-4, 4, -2, 2)], *x_steps, *y_steps, *z_steps[0]]
    near += [place(yy, z, x, other) for yy in (lax.rem(y + 1, Y), lax.rem(y + Y - 1, Y))]
    near += [place(y, zz, x, other) for zz in (lax.rem(z + 1, Z), lax.rem(z + Z - 1, Z))]
    near.append(sib)
    for device in near:
        greet(device)

    def wave_out(k):
        for device in waves[k]:
            pl.semaphore_signal(wave.at[k], inc=1, device_id=device, device_id_type=MESH)

    def wave_in(k):
        pl.semaphore_wait(wave.at[k], len(waves[k]))

    late = []
    loads = [
        pltpu.make_async_copy(do_hbm, do_all.at[c], load_sem.at[0]),
        pltpu.make_async_copy(o_hbm, o_own, load_sem.at[1]),
        pltpu.make_async_copy(q_hbm, q_all.at[c], load_sem.at[2]),
        pltpu.make_async_copy(k_hbm, kbuf.at[0], load_sem.at[3]),
        pltpu.make_async_copy(v_hbm, vbuf.at[0], load_sem.at[4]),
        pltpu.make_async_copy(lse_hbm, lse_ref, load_sem.at[6]),
        pltpu.make_async_copy(start_hbm, start_ref, load_sem.at[7]),
        pltpu.make_async_copy(vis_hbm, vis_ref, load_sem.at[8]),
    ]
    for load in loads:
        load.start()

    pl.semaphore_wait(barrier, len(near))

    cp_q = send(q_hbm, q_all.at[c], qx_s.at[0], qx_r.at[0], sib)
    cp_do = send(do_hbm, do_all.at[c], qx_s.at[1], qx_r.at[1], sib)
    cp_st = send(stat.at[c], stat.at[c], qx_s.at[2], qx_r.at[2], sib)
    cp_k, cp_v = [
        [send(src, buf.at[j], kv_s.at[2 * n + j - 1], kv_r.at[2 * n + j - 1], block_at(2 * j)) for j in (1, 2)]
        for n, (src, buf) in enumerate(((k_hbm, kbuf), (v_hbm, vbuf)))
    ]
    for copy in [*cp_k, *cp_v, cp_q, cp_do]:
        copy.start()

    def x_cols(yy, zz, cc):
        return x_hbm.at[:, pl.ds(pl.multiple_of(unit_owner(yy, zz) * UNIT + cc * HALF, HD), HALF)]

    x_own = pltpu.make_async_copy(x_cols(y, z, c), x_recv.at[named[0]], load_sem.at[5])
    x_own.start()
    cp_x = []
    for i, yy, zz, cc in peers:
        at = named[i]
        copy = send(x_cols(yy, zz, cc), x_recv.at[at], x_s.at[i * C + cc], x_r.at[at], place(yy, zz, x, cc))
        copy.start()
        cp_x.append(copy)

    for i in (0, 1, 5, 6, 7):
        loads[i].wait()
    for h in range(HQ):
        cols = pl.ds(h * HD, HD)
        prod = do_all[c, :, cols].astype(f32) * o_own[:, cols].astype(f32)
        stat[c, pl.ds(h, 1), :] = jnp.sum(prod.T, axis=0, keepdims=True)
    stat[c, pl.ds(HQ, HQ), :] = lse_ref[...] * LOG2E
    first = start_ref[...].astype(f32)
    for d in range(5):
        kb = block - d
        wanted = jnp.where(kb >= 0, kb, -7)
        hit = jnp.max(jnp.where(vis_ref[...] == wanted, 1.0, 0.0), axis=1, keepdims=True)
        stat[c, pl.ds(10 + d, 1), :] = jnp.where(hit > 0.5, first, FAR)
    stat[c, pl.ds(15, 1), :] = jnp.full((1, T), FAR, f32)
    cp_st.start()
    wave_out(0)

    for load in loads[2:5]:
        load.wait()
    cp_q.wait_recv()
    cp_do.wait_recv()
    cp_st.wait_recv()

    def row(r):
        return jnp.concatenate([stat[0, pl.ds(r, 1), :], stat[1, pl.ds(r, 1), :]], axis=1)


    def lowest(j):
        lows = []
        for i in range(C):
            d0, d1 = i + 2 * j, i - 1 + 2 * j
            at0, at1 = 10 + min(d0, 5), 10 + (d1 if d1 >= 0 else 5)
            lows.append(jnp.where(c == 0, stat[i, pl.ds(at0, 1), :], stat[i, pl.ds(at1, 1), :]))
        return jnp.concatenate(lows, axis=1)

    def heads(ref, h):
        return ref[:, :, pl.ds(h * HD, HD)].reshape(2 * T, HD)

    def probs(first, count):
        rows = pl.ds(first * T, count * T)
        iota_u = lax.broadcasted_iota(jnp.int32, (count * T, 2 * T), 0)
        iota_t = lax.broadcasted_iota(jnp.int32, (count * T, 2 * T), 1)
        key_pos = (block - 2 * first) * T + iota_u
        low = lowest(first)
        if count == 2:
            key_pos = jnp.where(iota_u < T, key_pos, key_pos - 3 * T)
            low = jnp.where(iota_u < T, low, lowest(first + 1))
        allowed = (key_pos.astype(f32) >= low) & (key_pos <= (block - c) * T + iota_t)
        key_rows = kbuf[first : first + count].reshape(count * T, HD)
        for h in range(HQ):
            s = dot(key_rows, heads(q_all, h), ((1,), (1,)))
            prob = jnp.where(allowed, jnp.exp2(s * (SCALE * LOG2E) - row(HQ + h)), 0.0)
            p_buf[h, rows, :] = prob
            p_half[h, rows, :] = prob.astype(bf16)
        part = jnp.zeros((count * T, HD), f32)
        for h in range(HQ):
            part += dot(p_half[h, rows, :], heads(do_all, h), ((1,), (0,)))
        return part

    def score_grads(first, count):
        rows = pl.ds(first * T, count * T)
        value_rows = vbuf[first : first + count].reshape(count * T, HD)
        for h in range(HQ):
            dp = dot(value_rows, heads(do_all, h), ((1,), (1,)))
            ds_buf[h, rows, :] = (p_buf[h, rows, :] * (dp - row(h)) * SCALE).astype(bf16)
        part = jnp.zeros((count * T, HD), f32)
        for h in range(HQ):
            part += dot(ds_buf[h, rows, :], heads(q_all, h), ((1,), (0,)))
        return part

    def give_back(n, part):
        for j in (1, 2):
            k = 2 * n + j - 1
            ret_send[k] = part[(j - 1) * T : j * T].astype(bf16)
            copy = send(ret_send.at[k], ret_recv.at[k], ret_s.at[k], ret_r.at[k], block_at(-2 * j))
            copy.start()
            cp_ret.append(copy)

    cp_ret = []
    own[0] = probs(0, 1)
    own[1] = score_grads(0, 1)
    wave_in(0)
    wave_out(1)
    for copy in cp_k:
        copy.wait_recv()
    give_back(0, probs(1, 2))
    for copy in cp_v:
        copy.wait_recv()
    give_back(1, score_grads(1, 2))

    wave_in(1)
    wave_out(2)
    key_cat = kbuf[...].reshape(3 * T, HD)
    for h in range(HQ):
        part = dot(ds_buf[h], key_cat, ((0,), (0,)))
        dq_part[0, :, pl.ds(h * HD, HD)] = part[:T]
        dq_part[1, :, pl.ds(h * HD, HD)] = part[T:]
    cp_dq = send(dq_part.at[other], dq_recv, dq_s.at[0], dq_r.at[0], sib)
    cp_dq.start()

    cp_g = []
    for n in range(2):
        cp_ret[2 * n].wait_recv()
        cp_ret[2 * n + 1].wait_recv()
        mine = g_all.at[n, named[0]]
        g_all[n, named[0]] = (own[n] + ret_recv[2 * n].astype(f32) + ret_recv[2 * n + 1].astype(f32)).astype(bf16)
        for i, yy, zz, cc in peers:
            at = named[i]
            copy = send(mine, g_all.at[n, at], g_s.at[n, i * C + cc], g_r.at[n, at], place(yy, zz, x, cc))
            copy.start()
            cp_g.append(copy)
        if n == 0:
            wave_in(2)
            wave_out(3)
            cp_dq.wait_recv()
            dq_ref[...] = (dq_part[c] + dq_recv[...]).astype(bf16)

    x_own.wait()
    for at in arrivals:
        send(x_recv.at[at], x_recv.at[at], x_s.at[0], x_r.at[at], sib).wait_recv()
    for m in range(C * GROUP):
        xt[m // 2, :, pl.ds(m % 2 * T, T)] = x_recv[m].T

    slot = z * X + x
    to_y = unit_owner(y, z)
    shares = (pl.ds(0, EARLY), pl.ds(EARLY, 2 * PAIR - EARLY))
    step = PAIR * X
    for n in range(2):
        for at in arrivals:
            send(g_all.at[n, at], g_all.at[n, at], g_s.at[n, 0], g_r.at[n, at], sib).wait_recv()
        if n == 0:
            wave_in(3)
        for i in range(Z // C):
            kz = lax.rem(z + 2 + i, Z // C)
            rows = pl.ds(pl.multiple_of(kz * step, step), step)
            total = dot(xt[0, rows, :], g_all[n, 0:2].reshape(2 * T, HD), ((1,), (0,)))
            for m in range(2, C * GROUP, 2):
                total += dot(xt[m // 2, rows, :], g_all[n, m : m + 2].reshape(2 * T, HD), ((1,), (0,)))
            acc[n, rows, :] = total
            for k in range(X):
                kx = lax.rem(x + 2 + k, X)
                m = kz * X + kx
                at = pl.multiple_of(m * PAIR, PAIR)
                if n == 0:
                    part = acc[0, pl.ds(at, EARLY), :]
                else:
                    left = acc[0, pl.ds(pl.multiple_of(at + EARLY, 8), PAIR - EARLY), :]
                    part = jnp.concatenate([left, acc[1, pl.ds(at, PAIR), :]], axis=0)
                rs_send[m, shares[n], :] = part.astype(bf16)
                to = place(to_y, c * (Z // C) + kz, kx, c)
                send(rs_send.at[m, shares[n]], rs_recv.at[slot, shares[n]], rs_s.at[n], rs_r.at[n], to).start()

    def rs_left():
        for n, rows in enumerate(shares):
            some = rs_recv.at[pl.ds(0, Z // C * X), rows]
            send(rs_send.at[:, rows], some, rs_s.at[n], rs_r.at[n], sib).wait_send()

    late.append(rs_left)
    cp_w = send(wsum, wsum, w_s.at[0], w_r.at[0], sib)
    some_xy = pl.ds(1, Y * X - 1)
    all_xy = send(sq1.at[some_xy], sq1.at[some_xy], sq_s.at[0], sq_r.at[0], sib)
    some_zc = send(sq2.at[pl.ds(0, Z - 1)], sq2.at[pl.ds(0, Z - 1)], sq_s.at[1], sq_r.at[1], sib)
    all_zc = send(sq2, sq2, sq_s.at[1], sq_r.at[1], sib)

    def far_first(places):
        return sorted(places, key=lambda steps: -sum(min(k, size - k) for k, size in zip(steps, (Y, Z, X, C))))

    def send_xy():
        for i, (dy, _, dx, _) in enumerate(far_first([(dy, 0, dx, 0) for dy in range(Y) for dx in range(X)])[:-1]):
            to = place(lax.rem(y + dy, Y), z, lax.rem(x + dx, X), c)
            send(sq1.at[0], sq1.at[1 + i], sq_s.at[0], sq_r.at[0], to).start()

    def send_zc():
        for _, dz, _, dc in far_first([(0, dz, 0, dc) for dz in range(Z) for dc in range(C)])[:-1]:
            to = place(y, lax.rem(z + dz, Z), x, lax.rem(c + dc, C))
            send(sq2.at[z], sq2.at[z], sq_s.at[1], sq_r.at[1], to).start()

    @pl.when(taker)
    def _():
        squares = jnp.zeros((1, HD), f32)
        for n, rows in enumerate(shares):
            here = rs_recv.at[:, rows]
            send(here, here, rs_s.at[n], rs_r.at[n], sib).wait_recv()
            total = rs_recv[0, rows, :].astype(f32)
            for i in range(1, Z * X):
                total += rs_recv[i, rows, :].astype(f32)
            wsum[rows, :] = total
            squares += jnp.sum(total * total, axis=0, keepdims=True)
        cp_w.start()
        sq1[0] = squares
        send_xy()
        all_xy.wait_recv()
        sq2[z] = jnp.sum(sq1[...], axis=0)
        send_zc()

    @pl.when(jnp.logical_not(taker))
    def _():
        cp_w.wait_recv()

    def sums_left():
        @pl.when(taker)
        def _():
            cp_w.wait_send()
            all_xy.wait_send()
            for part in (pl.ds(0, Z), pl.ds(0, Z - 1)):
                send(sq2.at[part], sq2.at[part], sq_s.at[1], sq_r.at[1], sib).wait_send()

    late.append(sums_left)
    halves = []
    for k in range(C):
        at, then = pl.ds(k * ROWS, ROWS), pl.ds(PAIR + k * ROWS, ROWS)
        halves.append(jnp.concatenate([wsum[then, :], wsum[at, :]], axis=1))
    w_ref[...] = jnp.where(c == 0, halves[0], halves[1])
    pl.when(taker)(some_zc.wait_recv)
    pl.when(jnp.logical_not(taker))(all_zc.wait_recv)

    lanes = jnp.sum(sq2[...], axis=0)
    square_total = jnp.sum(lanes, axis=1, keepdims=True)
    limit = math.sqrt(D * 2 * HD)
    clip = jnp.minimum(1.0, limit / (jnp.sqrt(square_total) + 1e-6))
    w_ref[...] *= clip

    for copy in [cp_q, cp_do, cp_st, *cp_k, *cp_v, *cp_x, *cp_ret, cp_dq, *cp_g]:
        copy.wait_send()

    for wait in late:
        wait()


def on_device(queries, keys, values, attention_out, output_grad, log_norm, layer_input, doc_start, visible_blocks):
    hbm = pl.BlockSpec(memory_space=pl.ANY)
    dma = pltpu.SemaphoreType.DMA
    return pl.pallas_call(
        kernel,
        out_shape=(pltpu.VMEM((ROWS, 2 * HD), f32), pltpu.VMEM((T, HQ * HD), bf16)),
        in_specs=[hbm] * 9,
        out_specs=(pl.BlockSpec(memory_space=pltpu.VMEM),) * 2,
        scratch_shapes=[
            pltpu.VMEM((HQ, T), f32),
            pltpu.VMEM((1, T), jnp.int32),
            pltpu.VMEM((1, 5), jnp.int32),
            pltpu.VMEM((C, T, HQ * HD), bf16),
            pltpu.VMEM((C, T, HQ * HD), bf16),
            pltpu.VMEM((T, HQ * HD), bf16),
            pltpu.VMEM((3, T, HD), bf16),
            pltpu.VMEM((3, T, HD), bf16),
            pltpu.VMEM((C, 16, T), f32),
            pltpu.VMEM((HQ, 3 * T, 2 * T), f32),
            pltpu.VMEM((HQ, 3 * T, 2 * T), bf16),
            pltpu.VMEM((HQ, 3 * T, 2 * T), bf16),
            pltpu.VMEM((4, T, HD), bf16),
            pltpu.VMEM((4, T, HD), bf16),
            pltpu.VMEM((C, T, HQ * HD), f32),
            pltpu.VMEM((T, HQ * HD), f32),
            pltpu.VMEM((C * GROUP, T, HALF), bf16),
            pltpu.VMEM((GROUP, HALF, C * T), bf16),
            pltpu.VMEM((2, T, HD), f32),
            pltpu.VMEM((2, C * GROUP, T, HD), bf16),
            pltpu.VMEM((2, HALF, HD), f32),
            pltpu.VMEM((Z // C * X, 2 * PAIR, HD), bf16),
            pltpu.VMEM((Z * X, 2 * PAIR, HD), bf16),
            pltpu.VMEM((2 * PAIR, HD), f32),
            pltpu.VMEM((Y * X, 1, HD), f32),
            pltpu.VMEM((Z, 1, HD), f32),
            dma((9,)),
            dma((3,)),
            dma((3,)),
            dma((4,)),
            dma((4,)),
            dma((4,)),
            dma((4,)),
            dma((C * GROUP,)),
            dma((C * GROUP,)),
            dma((2, C * GROUP)),
            dma((2, C * GROUP)),
            dma((1,)),
            dma((1,)),
            dma((2,)),
            dma((2,)),
            dma((1,)),
            dma((1,)),
            dma((2,)),
            dma((2,)),
            pltpu.SemaphoreType.REGULAR((4,)),
        ],
        compiler_params=pltpu.CompilerParams(
            collective_id=0, has_side_effects=True, vmem_limit_bytes=56 * 2**20
        ),
        name="clip_attention_backward",
    )(
        queries,
        keys,
        values,
        attention_out,
        output_grad,
        log_norm,
        layer_input,
        doc_start.reshape(1, T),
        visible_blocks,
    )


def solution(mesh):
    both = ("inner", "outer")
    return jax.shard_map(
        on_device,
        mesh=mesh,
        in_specs=(
            P(both, None),
            P(both, None),
            P(both, None),
            P(both, None),
            P(both, None),
            P(None, both),
            P(both, None),
            P(both),
            P(both, None),
        ),
        out_specs=(P(both, None), P(both, None)),
        check_vma=False,
    )
```
